256 devices in a mesh: group: 8 (over z), prefix: 32 (over x, y, core).
Axes of the slice: x: 4, y: 4, z: 8, core: 2. Of those that a mesh axis runs over, the one named last changes fastest.
Arguments:
- queries: bfloat16 [4096, 64, 128], P('prefix', 'group'), may hold values from -41 to 41
- prefix_keys: bfloat16 [4096, 8, 128], P(('group', 'prefix')), may hold values from -5 to 5
- prefix_values: bfloat16 [4096, 8, 128], P(('group', 'prefix')), may hold values from -24 to 24
- out_grad: bfloat16 [4096, 64, 128], P('prefix', 'group'), may hold values from -6 to 6
- tile_mask: int32 [2, 32], replicated, may hold values 0 or 1
- lengths: int32 [2], replicated, may hold values from 1024 to 2048, as said below
Outputs:
- attended: bfloat16 [4096, 64, 128], P('prefix', 'group')
- query_grad: bfloat16 [4096, 64, 128], P('prefix', 'group')
- key_grad: float32 [4096, 8, 128], P(('group', 'prefix'))
- value_grad: float32 [4096, 8, 128], P(('group', 'prefix'))
The draws below stay inside these ranges and needn't reach their ends.
Inputs may be any that keep to these rules, and one draw needn't show every extreme that they name: `tile_mask`: a 0 or 1 flag for each completion and prompt tile. `lengths`: one completion has exactly 2048 tokens.
All inputs are finite; a program needn't handle non-finite values.
Results may differ from the reference program's by a relative error of at most 0.035.
Values may be sent and summed in bfloat16 or wider, within the bound.
A program may use at most 128 MiB of HBM per device.

```python
import math
import jax
import jax.numpy as jnp
from jax import lax

QH = 64
KVH = 8
HD = 128
PTILE = 128
CTOKENS = 4096
CLEN = 2048
COMPS = 2
PTOK = 4096
PTILES = 32


def shared_keys(key, twin_pairs):
    normal_part = jnp.clip(jax.random.normal(jax.random.fold_in(key, 11), (PTOK, KVH, HD), jnp.float32), -5.0, 5.0)
    base = normal_part
    rows = jnp.arange(PTOK)[:, None, None]
    twins = (rows % 2 == 1) & (rows < 2 * twin_pairs)
    return jnp.where(twins, 0.99 * jnp.roll(base, 1, axis=0), base)


def draw_prefix_keys(key, part):
    return shared_keys(key, 0).astype(jnp.bfloat16)


def draw_queries(key, part):
    key = jax.random.fold_in(key, 2)
    return jnp.clip(2.0 * jax.random.normal(key, (CTOKENS, QH, HD), jnp.float32), -12.0, 12.0).astype(jnp.bfloat16)


def draw_lengths(key, part):
    key = jax.random.fold_in(key, 7)
    base = jax.random.randint(key, (COMPS,), CLEN // 2, CLEN, dtype=jnp.int32)
    longest = jax.random.randint(jax.random.fold_in(key, 1), (), 0, COMPS, dtype=jnp.int32)
    slots = jnp.arange(COMPS, dtype=jnp.int32)
    return jnp.where(slots == longest, jnp.int32(CLEN), base).astype(jnp.int32)


def set_ends(entries, key, low, largest):
    place = [jax.random.randint(jax.random.fold_in(key, axis), (), 0, length) for axis, length in enumerate(entries.shape)]
    widest = entries.shape.index(max(entries.shape))
    next_to = place[:widest] + [(place[widest] + 1) % entries.shape[widest]] + place[widest + 1:]
    return entries.at[tuple(place)].set(low).at[tuple(next_to)].set(largest)


def block_levels(own_key, shape, shards, low, top_value):
    def one(axis_at, shards_of):
        steps = jax.random.uniform(jax.random.fold_in(jax.random.fold_in(own_key, 6), axis_at), (shards_of,), jnp.float32, low / len(shards), top_value / len(shards))
        return jnp.repeat(jnp.exp(steps), shape[axis_at] // shards_of).reshape((-1,) + (1,) * (len(shape) - axis_at - 1))

    gain = one(*shards[0])
    for cut in shards[1:]:
        gain = gain * one(*cut)
    return gain


def normal_values(stream_key, shape, scale, reach, cuts=(), kind=jnp.bfloat16):
    drawn = scale * jax.random.normal(stream_key, shape, jnp.float32)
    if cuts:
        drawn = drawn * block_levels(stream_key, shape, cuts, -0.22, 0.18)
    return jnp.clip(drawn, -reach, reach).astype(kind)


def setup_inputs(seed: int = 0) -> dict:
    streams_of = jax.random.split(jax.random.key(seed), 7)
    return {
        "queries": draw_queries(jax.random.fold_in(streams_of[6], 71), 0),
        "prefix_keys": draw_prefix_keys(jax.random.fold_in(streams_of[6], 71), 0),
        "prefix_values": normal_values(streams_of[2], (PTOK, KVH, HD), 4.0, 24.0, ((0, 256),)),
        "out_grad": normal_values(streams_of[3], (CTOKENS, QH, HD), 2.0, 6.0, ((0, 32), (1, 8))),
        "tile_mask": set_ends((jax.random.randint(streams_of[4], (COMPS, PTILES), 0, 2) < 1).astype(jnp.int32), jax.random.fold_in(streams_of[4], 1), 0, 1),
        "lengths": draw_lengths(jax.random.fold_in(streams_of[6], 71), 0),
    }


def reference(queries, prefix_keys, prefix_values, out_grad, tile_mask, lengths):
    ratio = QH // KVH
    inv_root = 1.0 / math.sqrt(HD)
    tok_index = jnp.arange(CTOKENS, dtype=jnp.int32)
    owner = tok_index // CLEN
    valid = tok_index % CLEN < lengths[owner]
    valid_f = valid.astype(jnp.float32)
    key_tile = jnp.arange(PTOK, dtype=jnp.int32) // PTILE
    seen = (tile_mask[owner][:, key_tile] == 1) | (key_tile == 0)[None, :]
    grad_keep = jnp.where(valid[:, None, None], out_grad, jnp.zeros_like(out_grad))

    def one_head(head):
        kv_index = head // ratio
        query_rows = queries[:, head]
        key_rows = prefix_keys[:, kv_index]
        value_rows = prefix_values[:, kv_index]
        grad_rows = grad_keep[:, head]
        score = jnp.dot(query_rows, key_rows.T, preferred_element_type=jnp.float32) * inv_root
        score = jnp.where(seen, score, -jnp.inf)
        row_top = lax.optimization_barrier(jnp.max(score, axis=1, keepdims=True))
        log_total = row_top + jnp.log(lax.optimization_barrier(jnp.sum(jnp.exp(score - row_top), axis=1, keepdims=True)))
        prob = jnp.exp(score - log_total)
        weights = prob.astype(jnp.bfloat16)
        mixed = jnp.dot(weights, value_rows, preferred_element_type=jnp.float32) * valid_f[:, None]
        offset = lax.optimization_barrier(jnp.sum(grad_rows.astype(jnp.float32) * mixed, axis=1, keepdims=True))
        value_dot = jnp.dot(grad_rows, value_rows.T, preferred_element_type=jnp.float32)
        dscore = (prob * (value_dot - offset)).astype(jnp.bfloat16)
        query_grad = (jnp.dot(dscore, key_rows, preferred_element_type=jnp.float32) * inv_root).astype(jnp.bfloat16)
        key_grad = jnp.dot(dscore.T, query_rows, preferred_element_type=jnp.float32) * inv_root
        value_grad = jnp.dot(weights.T, grad_rows, preferred_element_type=jnp.float32)
        return (mixed.astype(jnp.bfloat16), query_grad, key_grad, value_grad)
    stacked = lax.map(one_head, jnp.arange(QH, dtype=jnp.int32))
    attended = jnp.transpose(stacked[0], (1, 0, 2))
    query_grad = jnp.transpose(stacked[1], (1, 0, 2))
    key_grad = jnp.transpose(lax.optimization_barrier(jnp.sum(stacked[2].reshape(KVH, ratio, PTOK, HD), axis=1)), (1, 0, 2))
    value_grad = jnp.transpose(lax.optimization_barrier(jnp.sum(stacked[3].reshape(KVH, ratio, PTOK, HD), axis=1)), (1, 0, 2))
    return (attended, query_grad, key_grad, value_grad)
```

```python
import functools
import math

import jax
import jax.numpy as jnp
from jax import lax
from jax.experimental import pallas as pl
from jax.experimental.pallas import tpu as pltpu
from jax.sharding import PartitionSpec as P

F32, BF16 = jnp.float32, jnp.bfloat16
MESH = pl.DeviceIdType.MESH
NZ, NX = 8, 4


class Place:
    def __init__(self):
        self.z = lax.axis_index("group")
        p = lax.axis_index("prefix")
        self.x, self.y, self.c = p // 8, p // 2 % 4, p % 2
        c = self.c
        self.a = self.x + c * (self.y - self.x)
        self.b = self.y + c * (self.x - self.y)

    def xy(self, a, b):
        c = self.c
        return a + c * (b - a), b + c * (a - b)

    def at(self, a, b):
        x, y = self.xy(a, b)
        return (self.z, (x * 4 + y) * 2 + self.c)

    def chip(self, z, c):
        return (z, (self.x * 4 + self.y) * 2 + c)


def greet(me):
    barrier = pltpu.get_barrier_semaphore()
    a, b, z, c = me.a, me.b, me.z, me.c
    devs = [me.at((a + o) % 4, b) for o in (1, 2, 3)] + [me.at(a, (b + o) % 4) for o in (1, 2, 3)]
    devs += [me.chip((z + d) % NZ, (c + r) % 2) for d in range(NZ) for r in range(2) if d or r]
    for d in devs:
        pl.semaphore_signal(barrier, inc=1, device_id=d, device_id_type=MESH)
    pl.semaphore_wait(barrier, len(devs))


def rcopy(src, dst, ss, rs, dev):
    return pltpu.make_async_remote_copy(src_ref=src, dst_ref=dst, send_sem=ss, recv_sem=rs,
                                        device_id=dev, device_id_type=MESH)


def gather_kernel(k_ref, v_ref, kv, f32buf, sendbuf, z_send, z_recv,
                  a_send, a_recv, b_send, b_recv, s_send, s_recv):
    me = Place()
    a, b, z, c = me.a, me.b, me.z, me.c
    for i, ref in enumerate((k_ref, v_ref)):
        f32buf[i] = ref[...].astype(F32).reshape(128, 128)
    for i in range(2):
        for h in range(NZ):
            sendbuf[i, h] = f32buf[i, pl.ds(h, 16, stride=8), :].astype(BF16)
    greet(me)
    strip = pl.ds(pl.multiple_of(c * 16, 16), 16)
    for d in range(NZ):
        h = (z + d) % NZ
        for r in range(2):
            ct = (c + r) % 2
            src, dst = sendbuf.at[ct, h], kv.at[ct, z, me.x, me.y, strip]
            if d or r:
                rcopy(src, dst, z_send.at[r], z_recv, me.chip(h, ct)).start()
            else:
                pltpu.make_async_copy(src, dst, z_recv).start()

    def blk(i, j, lo=0, n=8):
        x, y = me.xy(i, j)
        return kv.at[c, pl.ds(lo, n), x, y]

    sib = me.chip(z, 1 - c)
    sends = []

    def send(ref, ss, rs, dev):
        cp = rcopy(ref, ref, ss, rs, dev)
        cp.start()
        sends.append(cp)

    def wait(ref, rs):
        pltpu.make_async_copy(ref, ref, rs).wait()

    def sibling(ref):
        rcopy(ref, ref, s_send, s_recv, sib).start()

    near = (3, 1, 2)

    def along_b(k):
        ref = blk((a + cols[k]) % 4, b)
        for i, o in enumerate(near):
            send(ref, b_send.at[i, k], b_recv.at[i, k], me.at(a, (b + 4 - o) % 4))
        sibling(ref)

    def arrived(k):
        for i, o in enumerate(near):
            ref = blk((a + cols[k]) % 4, (b + o) % 4)
            wait(ref, b_recv.at[i, k])
            sibling(ref)

    cols = (0, 3, 1, 2)
    own = blk(a, b)
    wait(own, z_recv)
    for i, o in enumerate(near):
        send(own, a_send.at[i], a_recv.at[i], me.at((a + 4 - o) % 4, b))
    along_b(0)
    for k in range(1, 4):
        wait(blk((a + cols[k]) % 4, b), a_recv.at[k - 1])
        along_b(k)
    for k in range(4):
        arrived(k)
    other = kv.at[1 - c]
    wait(other, s_recv)
    wait(sendbuf.at[0, pl.ds(0, 7)], z_send.at[0])
    wait(sendbuf.at[0], z_send.at[1])
    wait(other, s_send)
    for cp in sends:
        cp.wait_send()


def gather(keys, values, space=pl.ANY):
    vm = pl.BlockSpec(memory_space=pltpu.VMEM)
    dma = pltpu.SemaphoreType.DMA
    return pl.pallas_call(
        gather_kernel,
        out_shape=jax.ShapeDtypeStruct((2, NZ, NX, NX, 32, 128), BF16),
        in_specs=[vm, vm],
        out_specs=pl.BlockSpec(memory_space=space),
        scratch_shapes=[
            pltpu.VMEM((2, 128, 128), F32), pltpu.VMEM((2, NZ, 16, 128), BF16),
            dma((2,)), dma, dma((3,)), dma((3,)), dma((3, 4)), dma((3, 4)), dma, dma,
        ],
        compiler_params=pltpu.CompilerParams(collective_id=0, has_side_effects=True),
        name="gather_heads",
    )(keys, values)


def scatter_kernel(g_ref, out, sbuf, bbuf, abuf, w, zbuf, s_send, s_recv, b_send, b_recv,
                   a_send, a_recv, z_send, z_recv):
    me = Place()
    a, b, z, c = me.a, me.b, me.z, me.c
    sib = me.chip(z, 1 - c)
    greet(me)
    sends = []

    def blk(kind, da, db):
        x, y = me.xy((a + da) % 4, (b + db) % 4)
        return kind, slice(None), x, y

    def send(src, dst, ss, rs, dev):
        cp = rcopy(src, dst, ss, rs, dev)
        cp.start()
        sends.append(cp)

    def wait(ref, rs):
        pltpu.make_async_copy(ref, ref, rs).wait()

    steps = [(da, db) for db in (2, 1, 3, 0) for da in (2, 1, 3, 0)]
    for da, db in steps:
        oa = me.x + (1 - c) * (me.y - me.x)
        ob = me.y + (1 - c) * (me.x - me.y)
        ta, tb = (oa + da) % 4, (ob + db) % 4
        tx = ta + (1 - c) * (tb - ta)
        ty = tb + (1 - c) * (ta - tb)
        send(g_ref.at[1 - c, :, tx, ty], sbuf.at[da, db], s_send.at[da, db], s_recv.at[da, db], sib)

    def f32(v):
        return v.astype(F32)

    for da, db in steps:
        wait(sbuf.at[da, db], s_recv.at[da, db])
        if db:
            sbuf[da, db] = (f32(sbuf[da, db]) + f32(g_ref[blk(c, da, db)])).astype(BF16)
            send(sbuf.at[da, db], bbuf.at[db - 1, da], b_send.at[db - 1, da], b_recv.at[db - 1, da],
                 me.at(a, (b + db) % 4))
            continue
        for i in range(3):
            wait(bbuf.at[i, da], b_recv.at[i, da])
        total = f32(sbuf[da, db]) + f32(g_ref[blk(c, da, db)]) + f32(bbuf[0, da]) + f32(bbuf[1, da]) + f32(bbuf[2, da])
        if da:
            sbuf[da, db] = total.astype(BF16)
            send(sbuf.at[da, db], abuf.at[da - 1], a_send.at[da - 1], a_recv.at[da - 1], me.at((a + da) % 4, b))
            continue
        for i in range(3):
            wait(abuf.at[i], a_recv.at[i])
        total = total + f32(abuf[0]) + f32(abuf[1]) + f32(abuf[2])
        w[...] = total.astype(BF16)
    for d in range(NZ):
        t = (z + d) % NZ
        for r in range(2):
            ct = (c + r) % 2
            src, dst = w.at[t, pl.ds(pl.multiple_of(ct * 16, 16), 16)], zbuf.at[c, z]
            if d or r:
                rcopy(src, dst, z_send.at[r], z_recv, me.chip(t, ct)).start()
            else:
                pltpu.make_async_copy(src, dst, z_recv).start()
    wait(zbuf, z_recv)
    for i in range(2):
        for h in range(NZ):
            out[i, pl.ds(h, 16, stride=8), :] = f32(zbuf[i, h])
    wait(zbuf.at[0, pl.ds(0, 7)], z_send.at[0])
    wait(zbuf.at[0], z_send.at[1])
    for cp in sends:
        cp.wait_send()


def scatter(g):
    vm = pl.BlockSpec(memory_space=pltpu.VMEM)
    dma = pltpu.SemaphoreType.DMA
    return pl.pallas_call(
        scatter_kernel,
        out_shape=jax.ShapeDtypeStruct((2, 128, 128), F32),
        in_specs=[vm],
        out_specs=vm,
        scratch_shapes=[
            pltpu.VMEM((4, 4, NZ, 32, 128), BF16), pltpu.VMEM((3, 4, NZ, 32, 128), BF16),
            pltpu.VMEM((3, NZ, 32, 128), BF16), pltpu.VMEM((NZ, 32, 128), BF16), pltpu.VMEM((2, NZ, 16, 128), BF16),
            dma((4, 4)), dma((4, 4)), dma((3, 4)), dma((3, 4)), dma((3,)), dma((3,)), dma((2,)), dma,
        ],
        compiler_params=pltpu.CompilerParams(collective_id=1, has_side_effects=True, vmem_limit_bytes=32 * 2**20),
        name="scatter_heads",
    )(g)


TILE = 128
C2 = (1.0 / math.sqrt(128)) * math.log2(math.e)
IR = 1.0 / math.sqrt(128)
NT = (((1,), (1,)), ((), ()))


def dot(a, b):
    return jnp.dot(a, b, preferred_element_type=F32)


def dot_nt(a, b):
    return lax.dot_general(a, b, NT, preferred_element_type=F32)


def compute_kernel(mask_ref, nval_ref, q_ref, g_ref, kv_ref,
                   att_ref, qg_ref, kvg_ref,
                   kc, vo, s_buf, p_buf, m_buf, acc, qg_acc, g0, qT, gT, idx, *, chunk):
    R = q_ref.shape[0]
    T = mask_ref.shape[0]
    tpc = chunk // TILE
    nchunks = T // tpc
    def scan(t, n):
        seen = jnp.logical_or(mask_ref[t] == 1, t == 0)

        @pl.when(seen)
        def _():
            idx[n] = t
            kc[pl.ds(pl.multiple_of(n * TILE, TILE), TILE), :] = kv_ref[0, pl.ds(pl.multiple_of(t * TILE, TILE), TILE), :]
            vo[pl.ds(pl.multiple_of(n * TILE, TILE), TILE), 0:128] = kv_ref[1, pl.ds(pl.multiple_of(t * TILE, TILE), TILE), :]
            vo[pl.ds(pl.multiple_of(n * TILE, TILE), TILE), 128:256] = jnp.ones((TILE, 128), BF16)

        @pl.when(jnp.logical_not(seen))
        def _():
            kvg_ref[0, pl.ds(pl.multiple_of(t * TILE, TILE), TILE), :] = jnp.zeros((TILE, 128), BF16)
            kvg_ref[1, pl.ds(pl.multiple_of(t * TILE, TILE), TILE), :] = jnp.zeros((TILE, 128), BF16)
        return n + seen.astype(jnp.int32)

    n = lax.fori_loop(0, T, scan, jnp.int32(0))
    nc = (n + tpc - 1) // tpc

    def pad(t, _):
        kc[pl.ds(pl.multiple_of(t * TILE, TILE), TILE), :] = kv_ref[0, 0:TILE, :]
        vo[pl.ds(pl.multiple_of(t * TILE, TILE), TILE), :] = jnp.zeros((TILE, 256), BF16)
        return 0
    lax.fori_loop(n, nc * tpc, pad, 0)

    nrow = nval_ref[0] * 8
    rows = lax.broadcasted_iota(jnp.int32, (R, 128), 0)
    valid = rows < nrow
    g0[...] = jnp.where(valid, g_ref[...].astype(F32), 0.0).astype(BF16)

    m_buf[...] = jnp.full((R, 128), -jnp.inf, F32)

    def crow(c):
        return pl.ds(pl.multiple_of(c * chunk, chunk), chunk)

    RB = 256

    def ph1(c, _):
        kk = kc[crow(c), :]
        for r in range(0, R, RB):
            s = dot_nt(q_ref[r:r + RB, :], kk)
            s_buf[c, r:r + RB, :] = s
            mm = s[:, 0:128]
            for j in range(1, tpc):
                mm = jnp.maximum(mm, s[:, j * 128:(j + 1) * 128])
            m_buf[r:r + RB, :] = jnp.maximum(m_buf[r:r + RB, :], mm)
        return 0
    lax.fori_loop(0, nc, ph1, 0)
    m_buf[...] = jnp.broadcast_to(jnp.max(m_buf[...], axis=1, keepdims=True), (R, 128))

    acc[...] = jnp.zeros((R, 256), F32)

    def ph2(c, _):
        vv = vo[crow(c), :]
        for r in range(0, R, RB):
            m = m_buf[r:r + RB, 0:1]
            p = jnp.exp2((s_buf[c, r:r + RB, :] - m) * C2).astype(BF16)
            p_buf[c, r:r + RB, :] = p
            acc[r:r + RB, :] += dot(p, vv)
        return 0
    lax.fori_loop(0, nc, ph2, 0)

    l = acc[:, 128:256]
    rl = 1.0 / l
    mixed = jnp.where(valid, acc[:, 0:128] * rl, 0.0)
    att_ref[...] = mixed.astype(BF16)
    gf = g0[...].astype(F32)
    off = jnp.sum(gf * mixed, axis=1, keepdims=True)
    m_buf[...] = jnp.broadcast_to(off, (R, 128))
    qT[...] = jnp.transpose(q_ref[...].astype(F32) * (rl * IR)).astype(BF16)
    gT[...] = jnp.transpose(gf * rl).astype(BF16)
    qg_acc[...] = jnp.zeros((R, 128), F32)

    def unpad(t, _):
        kc[pl.ds(pl.multiple_of(t * TILE, TILE), TILE), :] = jnp.zeros((TILE, 128), BF16)
        return 0
    lax.fori_loop(n, nc * tpc, unpad, 0)

    def ph3(c, _):
        vv = vo[crow(c), 0:128]
        kk = kc[crow(c), :]
        kgT = jnp.zeros((128, chunk), F32)
        vgT = jnp.zeros((128, chunk), F32)
        for r in range(0, R, RB):
            vd = dot_nt(g0[r:r + RB, :], vv)
            p = p_buf[c, r:r + RB, :]
            ds = (p.astype(F32) * (vd - m_buf[r:r + RB, 0:1])).astype(BF16)
            qg_acc[r:r + RB, :] += dot(ds, kk)
            kgT += dot(qT[:, r:r + RB], ds)
            vgT += dot(gT[:, r:r + RB], p)
        kg = jnp.transpose(kgT).astype(BF16)
        vg = jnp.transpose(vgT).astype(BF16)
        for j in range(tpc):
            pos = c * tpc + j

            @pl.when(pos < n)
            def _():
                t = idx[pos]
                kvg_ref[0, pl.ds(pl.multiple_of(t * TILE, TILE), TILE), :] = kg[j * TILE:(j + 1) * TILE, :]
                kvg_ref[1, pl.ds(pl.multiple_of(t * TILE, TILE), TILE), :] = vg[j * TILE:(j + 1) * TILE, :]
        return 0
    lax.fori_loop(0, nc, ph3, 0)
    rl = 1.0 / acc[:, 128:256]
    qg_ref[...] = (qg_acc[...] * (rl * IR)).astype(BF16)


def compute(mask_row, nval, q, g, kv, chunk=512):
    R = q.shape[0]
    S = kv.shape[1]
    sm = pl.BlockSpec(memory_space=pltpu.SMEM)
    vm = pl.BlockSpec(memory_space=pltpu.VMEM)
    return pl.pallas_call(
        functools.partial(compute_kernel, chunk=chunk),
        out_shape=(jax.ShapeDtypeStruct((R, 128), BF16), jax.ShapeDtypeStruct((R, 128), BF16),
                   jax.ShapeDtypeStruct((2, S, 128), BF16)),
        in_specs=[sm, sm, vm, vm, vm],
        out_specs=(vm, vm, vm),
        scratch_shapes=[
            pltpu.VMEM((S, 128), BF16), pltpu.VMEM((S, 256), BF16),
            pltpu.VMEM((S // chunk, R, chunk), F32), pltpu.VMEM((S // chunk, R, chunk), BF16),
            pltpu.VMEM((R, 128), F32), pltpu.VMEM((R, 256), F32), pltpu.VMEM((R, 128), F32),
            pltpu.VMEM((R, 128), BF16), pltpu.VMEM((128, R), BF16), pltpu.VMEM((128, R), BF16),
            pltpu.SMEM((S // TILE,), jnp.int32),
        ],
        compiler_params=pltpu.CompilerParams(vmem_limit_bytes=60 * 2**20),
        name="attend",
    )(mask_row, nval, q, g, kv)


def on_device(queries, prefix_keys, prefix_values, out_grad, tile_mask, lengths):
    tok = queries.shape[0]
    span = 2048
    first = lax.axis_index("prefix") * tok
    comp = first // span
    nval = jnp.clip(lax.dynamic_index_in_dim(lengths, comp, 0, keepdims=True) - first % span, 0, tok)
    mask_row = lax.dynamic_index_in_dim(tile_mask, comp, 0, keepdims=False)
    kv = gather(prefix_keys, prefix_values).reshape(2, -1, 128)
    q, g = queries.reshape(-1, 128), out_grad.reshape(-1, 128)
    att, qg, kvg = compute(mask_row, nval, q, g, kv)
    out = scatter(kvg.reshape(2, NZ, NX, NX, 32, 128)).reshape(2, 16, 8, 128)
    return att.reshape(queries.shape), qg.reshape(queries.shape), out[0], out[1]


def solution(mesh):
    tokens, owned = P("prefix", "group", None), P(("group", "prefix"), None, None)
    return jax.shard_map(
        on_device,
        mesh=mesh,
        in_specs=(tokens, owned, owned, tokens, P(), P()),
        out_specs=(tokens, tokens, owned, owned),
        check_vma=False,
    )
```

```python
import functools
import math

import jax
import jax.numpy as jnp
from jax import lax
from jax.experimental import pallas as pl
from jax.experimental.pallas import tpu as pltpu
from jax.sharding import PartitionSpec as P

F32, BF16 = jnp.float32, jnp.bfloat16
MESH = pl.DeviceIdType.MESH
NZ = 8
BLK = 256
SPAN = 2048
ROOT = 1.0 / math.sqrt(128)
C2 = ROOT * math.log2(math.e)
HIDDEN = -1e30

STEPS = [(2, 2), (1, 1), (3, 3), (2, 1), (1, 2), (2, 3), (3, 2), (1, 3), (3, 1),
         (2, 0), (0, 2), (1, 0), (0, 1), (3, 0), (0, 3), (0, 0)]
FAR, NEAR = range(0, 9), range(9, 16)
RING = (3, 1, 2)
COLS = (0, 3, 1, 2)


class Place:
    def __init__(self):
        self.z = lax.axis_index("group")
        p = lax.axis_index("prefix")
        self.x, self.y, self.c = p // 8, p // 2 % 4, p % 2
        self.a, self.b = self.turn(self.x, self.y)

    def turn(self, u, v):
        return u + self.c * (v - u), v + self.c * (u - v)

    def turn_other(self, u, v):
        return u + (1 - self.c) * (v - u), v + (1 - self.c) * (u - v)

    def at(self, a, b):
        x, y = self.turn(a, b)
        return (self.z, (x * 4 + y) * 2 + self.c)

    def chip(self, z, c):
        return (z, (self.x * 4 + self.y) * 2 + c)


def rcopy(src, dst, ss, rs, dev):
    return pltpu.make_async_remote_copy(src_ref=src, dst_ref=dst, send_sem=ss, recv_sem=rs,
                                        device_id=dev, device_id_type=MESH)


def wait(ref, sem):
    pltpu.make_async_copy(ref, ref, sem).wait()


def dot(u, v):
    return jnp.dot(u, v, preferred_element_type=F32)


def dot_nt(u, v):
    return lax.dot_general(u, v, (((1,), (1,)), ((), ())), preferred_element_type=F32)


def f32(v):
    return v.astype(F32)


def over(ns, body):
    ns = list(ns)
    straight = ns == list(range(ns[0], ns[0] + len(ns)))
    codes = (0 if straight else sum(n * 16**i for i, n in enumerate(ns)),
             sum(STEPS[n][0] * 4**i for i, n in enumerate(ns)),
             sum(STEPS[n][1] * 4**i for i, n in enumerate(ns)))

    def one(i, carry):
        cn, cx, cy = carry
        body(ns[0] + i if straight else lax.rem(cn, 16), lax.rem(cx, 4), lax.rem(cy, 4))
        return lax.div(cn, 16), lax.div(cx, 4), lax.div(cy, 4)

    lax.fori_loop(0, len(ns), one, tuple(jnp.int32(v) for v in codes))


def kernel(mask_ref, len_ref, q_hbm, g_hbm, k_hbm, v_hbm, attv, qgv, zbuf,
           kin, vin, q, g, strips, sendbuf, kv, vo, kord, bias, s_buf, vd_buf, p_buf, m_part, m_near, m_all,
           off, acc_near, acc, qTf, gTf, qT, gT, gbuf, sbuf, bbuf, abuf, w,
           in_sem, z_send, z_recv, a_send, a_recv, b_send, b_recv, s_send, s_recv,
           rs_send, rs_recv, rb_send, rb_recv, ra_send, ra_recv, rz_send, rz_recv):
    me = Place()
    a, b, z, c = me.a, me.b, me.z, me.c
    R = q.shape[0]
    RB = 256
    sib = me.chip(z, 1 - c)
    ins = [pltpu.make_async_copy(s, d, in_sem.at[i])
           for i, (s, d) in enumerate(((k_hbm, kin), (v_hbm, vin), (q_hbm, q), (g_hbm, g)))]
    for cp in ins:
        cp.start()
    barrier = pltpu.get_barrier_semaphore()
    partners = [me.at((a + o) % 4, b) for o in (1, 2, 3)] + [me.at(a, (b + o) % 4) for o in (1, 2, 3)]
    partners += [me.chip((z + d) % NZ, (c + r) % 2) for d in range(NZ) for r in range(2) if d or r]
    for dev in partners:
        pl.semaphore_signal(barrier, inc=1, device_id=dev, device_id_type=MESH)
    ins[0].wait()
    ins[1].wait()
    for i, ref in enumerate((kin, vin)):
        strips[i] = f32(ref[...]).reshape(128, 128)
    for i in range(2):
        for h in range(NZ):
            sendbuf[i, h] = strips[i, pl.ds(h, 16, stride=8), :].astype(BF16)
    pl.semaphore_wait(barrier, len(partners))

    strip = pl.ds(pl.multiple_of(c * 16, 16), 16)
    for d in range(NZ):
        h = (z + d) % NZ
        for r in range(2):
            ct = (c + r) % 2
            src, dst = sendbuf.at[ct, h], kv.at[ct, z, me.x, me.y, strip]
            if d or r:
                rcopy(src, dst, z_send.at[r], z_recv, me.chip(h, ct)).start()
            else:
                pltpu.make_async_copy(src, dst, z_recv).start()

    ins[2].wait()
    ins[3].wait()
    comp = lax.axis_index("prefix") * (R // 8) // SPAN
    nrow = (len_ref[comp] - lax.axis_index("prefix") * (R // 8) % SPAN) * 8
    valid = lax.broadcasted_iota(jnp.int32, (R, 128), 0) < nrow
    g[...] = jnp.where(valid, f32(g[...]), 0.0).astype(BF16)
    vo[:, 128:256] = jnp.ones((vo.shape[0], 128), BF16)
    lane = lax.broadcasted_iota(jnp.int32, (8, BLK), 1) // 32
    for x in range(4):
        row = jnp.zeros((8, BLK), F32)
        for zz in range(NZ):
            t = zz * 4 + x
            if t:
                level = (1.0 - mask_ref[comp, t].astype(F32)) * HIDDEN
                row = jnp.where(lane == zz, level, row)
        bias[x] = row
    m_part[...] = jnp.full((R, 128), -jnp.inf, F32)
    qTf[...] = jnp.transpose(f32(q[...]))
    gTf[...] = jnp.transpose(f32(g[...]))

    def mirror(n):
        pair = 1 - 2 * lax.rem(n + 1, 2)
        return jnp.where((n < 3) | (n == 15), n, n + pair)

    def block(dx, dy):
        return (me.x + dx) % 4, (me.y + dy) % 4

    def at_pos(n):
        return pl.ds(pl.multiple_of(n * BLK, BLK), BLK)

    def scores_and_dots(n, dx, dy):
        x, y = block(dx, dy)
        k = kv[0, :, x, y].reshape(BLK, 128)
        kord[at_pos(n), :] = k
        x2, y2 = block(dy, dx)
        n2 = mirror(n)
        v = kv[1, :, x2, y2].reshape(BLK, 128)
        vo[at_pos(n2), 0:128] = v
        for r in range(0, R, RB):
            s = dot_nt(q[r:r + RB, :], k)
            s = (s.reshape(RB // 8, 8, BLK) + bias[x][None]).reshape(RB, BLK)
            s_buf[n, r:r + RB, :] = s
            m_part[r:r + RB, :] = jnp.maximum(m_part[r:r + RB, :], jnp.maximum(s[:, :128], s[:, 128:]))
            vd_buf[n2, r:r + RB, :] = dot_nt(g[r:r + RB, :], v)

    def weights(m_ref):
        def one(n, dx, dy):
            for r in range(0, R, RB):
                m = m_ref[r:r + RB, :]
                for j in range(2):
                    p = jnp.exp2((s_buf[n, r:r + RB, 128 * j:128 * j + 128] - m) * C2)
                    p_buf[r:r + RB, pl.ds(pl.multiple_of(n * BLK + 128 * j, 128), 128)] = p.astype(BF16)
        return one

    def top(ref):
        ref[...] = jnp.broadcast_to(jnp.max(m_part[...], axis=1, keepdims=True), (R, 128))

    sends = []

    def send(ref, ss, rs, dev):
        cp = rcopy(ref, ref, ss, rs, dev)
        cp.start()
        sends.append(cp)

    def blk(da, db):
        x, y = me.turn((a + da) % 4, (b + db) % 4)
        return kv.at[c, :, x, y]

    def hand_over(da, db):
        dx, dy = me.turn(jnp.int32(da), jnp.int32(db))
        send(blk(da, db), s_send.at[da, db], s_recv.at[dx, dy], sib)

    def handed(da, db):
        dx, dy = me.turn_other(jnp.int32(da), jnp.int32(db))
        x, y = block(dx, dy)
        wait(kv.at[1 - c, :, x, y], s_recv.at[dx, dy])

    def along_b(k):
        for i, o in enumerate(RING):
            send(blk(COLS[k], 0), b_send.at[i, k], b_recv.at[i, k], me.at(a, (b + 4 - o) % 4))
        hand_over(COLS[k], 0)

    def arrived(k):
        for i, o in enumerate(RING):
            wait(blk(COLS[k], o), b_recv.at[i, k])
            hand_over(COLS[k], o)

    wait(blk(0, 0), z_recv)
    for i, o in enumerate(RING):
        send(blk(0, 0), a_send.at[i], a_recv.at[i], me.at((a + 4 - o) % 4, b))
    along_b(0)
    for k in range(1, 4):
        wait(blk(COLS[k], 0), a_recv.at[k - 1])
        along_b(k)
    arrived(0)
    for k in range(4):
        handed(COLS[k], 0)
    for o in RING:
        handed(0, o)
    over(NEAR, scores_and_dots)
    top(m_near)
    arrived(1)
    over(NEAR, weights(m_near))
    lo = NEAR[0] * BLK
    for r in range(0, R, RB):
        acc_near[r:r + RB, :] = dot(p_buf[r:r + RB, lo:], vo[lo:, :])
    for k in range(1, 4):
        if k > 1:
            arrived(k)
        for o in RING:
            handed(COLS[k], o)
        over([n for n in FAR if STEPS[n][0] == COLS[k]], scores_and_dots)
    top(m_all)
    over(FAR, weights(m_all))
    for r in range(0, R, RB):
        rows = slice(r, r + RB)
        f = jnp.exp2((m_near[rows, :] - m_all[rows, :]) * C2)
        m_near[rows, :] = f
        part = dot(p_buf[rows, :lo], vo[:lo, :])
        total = part[:, :128] + f * acc_near[rows, :128]
        rl = 1.0 / (part[:, 128:] + f * acc_near[rows, 128:])
        mixed = jnp.where(valid[rows, :], total * rl, 0.0)
        attv[rows, :] = mixed.astype(BF16)
        off[rows, :] = jnp.broadcast_to(jnp.sum(f32(g[rows, :]) * mixed, axis=1, keepdims=True), (RB, 128))
        m_all[rows, :] = rl
        rlT = jnp.transpose(rl)
        fT = jnp.transpose(f)
        qs = qTf[:, rows] * (rlT * ROOT)
        gs = gTf[:, rows] * rlT
        qT[0, :, rows] = qs.astype(BF16)
        qT[1, :, rows] = (qs * fT).astype(BF16)
        gT[0, :, rows] = gs.astype(BF16)
        gT[1, :, rows] = (gs * fT).astype(BF16)

    def part_sum(n):
        wait(sbuf.at[n], rs_recv.at[n])
        return f32(sbuf[n]) + f32(gbuf[n, c])

    def to_b(n, dx, dy):
        da, db = me.turn(dx, dy)

        @pl.when(db != 0)
        def _():
            sbuf[n] = part_sum(n).astype(BF16)
            rcopy(sbuf.at[n], bbuf.at[db - 1, da], rb_send.at[db - 1, da], rb_recv.at[db - 1, da],
                  me.at(a, (b + db) % 4)).start()

    def gradients(n, dx, dy):
        far = lax.div(n, 9)
        cols = at_pos(n)
        kg, vg = jnp.zeros((128, BLK), F32), jnp.zeros((128, BLK), F32)
        for r in range(0, R, RB):
            rows = slice(r, r + RB)
            p = p_buf[rows, cols]
            o = jnp.concatenate([off[rows, :]] * 2, axis=1)
            ds = (f32(p) * (vd_buf[n, rows, :] - o)).astype(BF16)
            p_buf[rows, cols] = ds
            kg += dot(qT[far, :, rows], ds)
            vg += dot(gT[far, :, rows], p)
        gbuf[n, 0] = jnp.transpose(kg).astype(BF16).reshape(NZ, 32, 128)
        gbuf[n, 1] = jnp.transpose(vg).astype(BF16).reshape(NZ, 32, 128)
        rcopy(gbuf.at[n, 1 - c], sbuf.at[n], rs_send.at[n], rs_recv.at[n], sib).start()

    LAG = 2

    codes = tuple(sum(s[i] * 4**j for j, s in enumerate(STEPS)) for i in range(2))

    def one(n, carry):
        cx, cy, ox, oy = carry
        dx, dy = lax.rem(cx, 4), lax.rem(cy, 4)
        gradients(n, dx, dy)

        @pl.when(n >= LAG)
        def _():
            to_b(n - LAG, lax.rem(ox, 4), lax.rem(oy, 4))
        step = jnp.where(n >= LAG, 4, 1)
        return lax.div(cx, 4), lax.div(cy, 4), lax.div(ox, step), lax.div(oy, step)

    lax.fori_loop(0, 16, one, tuple(jnp.int32(v) for v in codes + codes))
    for n in range(16 - LAG, 15):
        to_b(n, jnp.int32(STEPS[n][0]), jnp.int32(STEPS[n][1]))

    for r in range(0, R, RB):
        rows = slice(r, r + RB)
        t = dot(p_buf[rows, :lo], kord[:lo, :]) + m_near[rows, :] * dot(p_buf[rows, lo:], kord[lo:, :])
        qgv[rows, :] = (t * (m_all[rows, :] * ROOT)).astype(BF16)

    tail = []
    for n in NEAR:
        dx, dy = STEPS[n]
        if dx and not dy:
            da = dx
            m = n + c * (STEPS.index((0, dx)) - n)
            total = part_sum(m)
            for i in range(3):
                wait(bbuf.at[i, da], rb_recv.at[i, da])
                total = total + f32(bbuf[i, da])
            sbuf[m] = total.astype(BF16)
            cp = rcopy(sbuf.at[m], abuf.at[da - 1], ra_send.at[da - 1], ra_recv.at[da - 1], me.at((a + da) % 4, b))
            cp.start()
            tail.append(cp)
    total = part_sum(15)
    for i in range(3):
        wait(bbuf.at[i, 0], rb_recv.at[i, 0])
        total = total + f32(bbuf[i, 0])
    for i in range(3):
        wait(abuf.at[i], ra_recv.at[i])
        total = total + f32(abuf[i])
    w[...] = total.astype(BF16)
    for d in range(NZ):
        t = (z + d) % NZ
        for r in range(2):
            ct = (c + r) % 2
            src, dst = w.at[t, pl.ds(pl.multiple_of(ct * 16, 16), 16)], zbuf.at[c, z]
            if d or r:
                rcopy(src, dst, rz_send.at[r], rz_recv, me.chip(t, ct)).start()
            else:
                pltpu.make_async_copy(src, dst, rz_recv).start()
    for cp in sends + tail:
        cp.wait_send()
    wait(sendbuf.at[0, pl.ds(0, 7)], z_send.at[0])
    wait(sendbuf.at[0], z_send.at[1])
    for n in range(16):
        wait(gbuf.at[n, 0], rs_send.at[n])
    for i in range(3):
        for j in range(4):
            wait(bbuf.at[i, j], rb_send.at[i, j])
    wait(zbuf, rz_recv)
    wait(zbuf.at[0, pl.ds(0, 7)], rz_send.at[0])
    wait(zbuf.at[0], rz_send.at[1])


def write_kernel(att_in, qg_in, zbuf, att, qg, kg, vg, buf, sem):
    cps = [pltpu.make_async_copy(att_in, att, sem.at[0]), pltpu.make_async_copy(qg_in, qg, sem.at[1])]
    for cp in cps:
        cp.start()
    for i, dst in enumerate((kg, vg)):
        for h in range(NZ):
            buf[i, pl.ds(h, 16, stride=8), :] = f32(zbuf[i, h])
        cps.append(pltpu.make_async_copy(buf.at[i], dst, sem.at[2 + i]))
        cps[-1].start()
    for cp in cps:
        cp.wait()


def on_device(queries, prefix_keys, prefix_values, out_grad, tile_mask, lengths):
    R = queries.shape[0] * queries.shape[1]
    S = 16 * BLK
    sm, hbm = pl.BlockSpec(memory_space=pltpu.SMEM), pl.BlockSpec(memory_space=pl.ANY)
    vmem, dma = pltpu.VMEM, pltpu.SemaphoreType.DMA
    rows = jax.ShapeDtypeStruct((R, 128), BF16)
    att, qg, heads = pl.pallas_call(
        kernel,
        out_shape=(rows, rows, jax.ShapeDtypeStruct((2, NZ, 16, 128), BF16)),
        in_specs=[sm, sm, hbm, hbm, hbm, hbm],
        out_specs=(pl.BlockSpec(memory_space=vmem),) * 3,
        scratch_shapes=[
            vmem((16, 8, 128), BF16), vmem((16, 8, 128), BF16), vmem((R, 128), BF16), vmem((R, 128), BF16),
            vmem((2, 128, 128), F32), vmem((2, NZ, 16, 128), BF16), vmem((2, NZ, 4, 4, 32, 128), BF16),
            vmem((S, 256), BF16), vmem((S, 128), BF16), vmem((4, 8, BLK), F32),
            vmem((16, R, BLK), F32), vmem((16, R, BLK), F32), vmem((R, S), BF16),
            vmem((R, 128), F32), vmem((R, 128), F32), vmem((R, 128), F32),
            vmem((R, 128), F32), vmem((R, 256), F32), vmem((8, 128), F32),
            vmem((128, R), F32), vmem((128, R), F32), vmem((2, 128, R), BF16), vmem((2, 128, R), BF16),
            vmem((16, 2, NZ, 32, 128), BF16), vmem((16, NZ, 32, 128), BF16), vmem((3, 4, NZ, 32, 128), BF16),
            vmem((3, NZ, 32, 128), BF16), vmem((NZ, 32, 128), BF16),
            dma((4,)), dma((2,)), dma, dma((3,)), dma((3,)), dma((3, 4)), dma((3, 4)),
            dma((4, 4)), dma((4, 4)), dma((16,)), dma((16,)), dma((3, 4)), dma((3, 4)), dma((3,)), dma((3,)),
            dma((2,)), dma,
        ],
        compiler_params=pltpu.CompilerParams(collective_id=0, has_side_effects=True,
                                             vmem_limit_bytes=60 * 2**20),
        name="shared_prompt",
    )(tile_mask, lengths, queries.reshape(R, 128), out_grad.reshape(R, 128), prefix_keys, prefix_values)
    grads = jax.ShapeDtypeStruct((128, 128), F32)
    att, qg, kg, vg = pl.pallas_call(
        write_kernel,
        out_shape=(rows, rows, grads, grads),
        in_specs=[pl.BlockSpec(memory_space=vmem)] * 3,
        out_specs=(hbm, hbm, hbm, hbm),
        scratch_shapes=[vmem((2, 128, 128), F32), dma((4,))],
        name="write_out",
    )(att, qg, heads)
    shape = prefix_keys.shape
    return att.reshape(queries.shape), qg.reshape(queries.shape), kg.reshape(shape), vg.reshape(shape)


def solution(mesh):
    tokens, owned = P("prefix", "group", None), P(("group", "prefix"), None, None)
    return jax.shard_map(
        on_device,
        mesh=mesh,
        in_specs=(tokens, owned, owned, tokens, P(), P()),
        out_specs=(tokens, tokens, owned, owned),
        check_vma=False,
    )
```

```python
import functools
import math

import jax
import jax.numpy as jnp
from jax import lax
from jax.experimental import pallas as pl
from jax.experimental.pallas import tpu as pltpu
from jax.sharding import PartitionSpec as P

F32, BF16 = jnp.float32, jnp.bfloat16
MESH = pl.DeviceIdType.MESH
NZ = 8
BLK = 256
SPAN = 2048
ROOT = 1.0 / math.sqrt(128)
C2 = ROOT * math.log2(math.e)
HIDDEN = -1e30

STEPS = [(2, 2), (2, 1), (1, 2), (2, 3), (3, 2), (1, 1), (1, 3), (3, 1), (3, 3),
         (2, 0), (0, 2), (1, 0), (0, 1), (3, 0), (0, 3), (0, 0)]
FAR, NEAR = range(0, 9), range(9, 16)
RING = (3, 1, 2)
COLS = (0, 3, 1, 2)


class Place:
    def __init__(self):
        self.z = lax.axis_index("group")
        p = lax.axis_index("prefix")
        self.x, self.y, self.c = p // 8, p // 2 % 4, p % 2
        self.a, self.b = self.turn(self.x, self.y)

    def turn(self, u, v):
        return u + self.c * (v - u), v + self.c * (u - v)

    def turn_other(self, u, v):
        return u + (1 - self.c) * (v - u), v + (1 - self.c) * (u - v)

    def at(self, a, b):
        x, y = self.turn(a, b)
        return (self.z, (x * 4 + y) * 2 + self.c)

    def chip(self, z, c):
        return (z, (self.x * 4 + self.y) * 2 + c)


def rcopy(src, dst, ss, rs, dev):
    return pltpu.make_async_remote_copy(src_ref=src, dst_ref=dst, send_sem=ss, recv_sem=rs,
                                        device_id=dev, device_id_type=MESH)


def wait(ref, sem):
    pltpu.make_async_copy(ref, ref, sem).wait()


def dot(u, v):
    return jnp.dot(u, v, preferred_element_type=F32)


def dot_nt(u, v):
    return lax.dot_general(u, v, (((1,), (1,)), ((), ())), preferred_element_type=F32)


def f32(v):
    return v.astype(F32)


def over(ns, body):
    ns = list(ns)
    straight = ns == list(range(ns[0], ns[0] + len(ns)))
    codes = (0 if straight else sum(n * 16**i for i, n in enumerate(ns)),
             sum(STEPS[n][0] * 4**i for i, n in enumerate(ns)),
             sum(STEPS[n][1] * 4**i for i, n in enumerate(ns)))

    def one(i, carry):
        cn, cx, cy = carry
        body(ns[0] + i if straight else lax.rem(cn, 16), lax.rem(cx, 4), lax.rem(cy, 4))
        return lax.div(cn, 16), lax.div(cx, 4), lax.div(cy, 4)

    lax.fori_loop(0, len(ns), one, tuple(jnp.int32(v) for v in codes))


def each(ns, body):
    for n in ns:
        body(n, *STEPS[n])


def pick(n, values):
    out = jnp.int32(values[0])
    for i, v in enumerate(values[1:], 1):
        out = jnp.where(n == i, v, out)
    return out


def kernel(mask_ref, len_ref, q_hbm, g_hbm, k_hbm, v_hbm, attv, qgv, zbuf,
           kin, vin, q, g, strips, sendbuf, kv, vo, kord, bias, s_buf, vd_buf, p_buf, m_part, m_near, m_all,
           off, acc_near, qTf, gTf, qT, gT, gbuf, sbuf, bbuf, abuf, w,
           in_sem, z_send, z_self, z_recv, a_send, a_recv, b_send, b_recv, s_send, s_recv,
           rs_send, rs_recv, rb_send, rb_recv, ra_send, ra_recv, rz_send, rz_self, rz_recv):
    me = Place()
    a, b, z, c = me.a, me.b, me.z, me.c
    R = q.shape[0]
    RB = 256
    K, V = 0, 1
    sib = me.chip(z, 1 - c)
    mine, others = pl.ds(pl.multiple_of(c * 4, 4), 4), pl.ds(pl.multiple_of(4 - c * 4, 4), 4)
    my_half = lax.div(z, 4)
    ins = [pltpu.make_async_copy(s, d, in_sem.at[i])
           for i, (s, d) in enumerate(((k_hbm, kin), (v_hbm, vin), (q_hbm, q), (g_hbm, g)))]
    for cp in ins:
        cp.start()
    barrier = pltpu.get_barrier_semaphore()
    partners = [me.at((a + o) % 4, b) for o in (1, 2, 3)] + [me.at(a, (b + o) % 4) for o in (1, 2, 3)]
    partners += [me.chip((z + d) % NZ, (c + r) % 2) for d in range(NZ) for r in range(2) if d or r]
    for dev in partners:
        pl.semaphore_signal(barrier, inc=1, device_id=dev, device_id_type=MESH)
    for i, ref in enumerate((kin, vin)):
        ins[i].wait()
        strips[i] = f32(ref[...]).reshape(128, 128)
        for h in range(NZ):
            sendbuf[i, h] = strips[i, pl.ds(h, 16, stride=8), :].astype(BF16)
    pl.semaphore_wait(barrier, len(partners))

    def to_or_keep(src, dst, ss, rs, here, dev):
        @pl.when(here)
        def _():
            pltpu.make_async_copy(src, dst, rs).start()

        @pl.when(jnp.logical_not(here))
        def _():
            rcopy(src, dst, ss, rs, dev).start()

    strip = pl.ds(pl.multiple_of(c * 16, 16), 16)
    for i in (K, V):
        dst = kv.at[i, z, me.x, me.y, strip]
        for d in range(1, NZ):
            h = (z + d) % NZ
            rcopy(sendbuf.at[i, h], dst, z_send.at[i], z_recv.at[i], me.chip(h, my_half)).start()
        to_or_keep(sendbuf.at[i, z], dst, z_self.at[i], z_recv.at[i], my_half == c, sib)

    ins[2].wait()
    ins[3].wait()
    comp = lax.axis_index("prefix") * (R // 8) // SPAN
    nrow = (len_ref[comp] - lax.axis_index("prefix") * (R // 8) % SPAN) * 8
    valid = lax.broadcasted_iota(jnp.int32, (R, 128), 0) < nrow
    g[...] = jnp.where(valid, f32(g[...]), 0.0).astype(BF16)
    vo[:, 128:256] = jnp.ones((vo.shape[0], 128), BF16)
    lane = lax.broadcasted_iota(jnp.int32, (8, BLK), 1) // 32
    for x in range(4):
        row = jnp.zeros((8, BLK), F32)
        for zz in range(NZ):
            t = zz * 4 + x
            if t:
                level = (1.0 - mask_ref[comp, t].astype(F32)) * HIDDEN
                row = jnp.where(lane == zz, level, row)
        bias[x] = row
    m_part[...] = jnp.full((R, 128), -jnp.inf, F32)

    def block(dx, dy):
        return (me.x + dx) % 4, (me.y + dy) % 4

    def at_pos(n):
        return pl.ds(n * BLK if isinstance(n, int) else pl.multiple_of(n * BLK, BLK), BLK)

    def scores(n, dx, dy):
        x, y = block(dx, dy)
        k = kv[K, :, x, y].reshape(BLK, 128)
        kord[at_pos(n), :] = k
        for r in range(0, R, RB):
            s = dot_nt(q[r:r + RB, :], k)
            s = (s.reshape(RB // 8, 8, BLK) + bias[x][None]).reshape(RB, BLK)
            s_buf[n, r:r + RB, :] = s
            m_part[r:r + RB, :] = jnp.maximum(m_part[r:r + RB, :], jnp.maximum(s[:, :128], s[:, 128:]))

    def values_in(n, dx, dy):
        x, y = block(dx, dy)
        vo[at_pos(n), 0:128] = kv[V, :, x, y].reshape(BLK, 128)

    def value_dots(n, dx, dy):
        v = vo[at_pos(n), 0:128]
        for r in range(0, R, RB):
            vd_buf[n, r:r + RB, :] = dot_nt(g[r:r + RB, :], v)

    def weights(m_ref):
        def one(n, dx, dy):
            for r in range(0, R, RB):
                m = m_ref[r:r + RB, :]
                for j in range(2):
                    p = jnp.exp2((s_buf[n, r:r + RB, 128 * j:128 * j + 128] - m) * C2)
                    p_buf[r:r + RB, pl.ds(pl.multiple_of(n * BLK + 128 * j, 128), 128)] = p.astype(BF16)
        return one

    def top(ref):
        ref[...] = jnp.broadcast_to(jnp.max(m_part[...], axis=1, keepdims=True), (R, 128))

    sends = []

    def send(ref, ss, rs, dev):
        cp = rcopy(ref, ref, ss, rs, dev)
        cp.start()
        sends.append(cp)

    def blk(i, da, db):
        x, y = me.turn((a + da) % 4, (b + db) % 4)
        return kv.at[i, mine, x, y]

    def hand_over(i, da, db):
        dx, dy = me.turn(jnp.int32(da), jnp.int32(db))
        send(blk(i, da, db), s_send.at[i, da, db], s_recv.at[i, dx, dy], sib)

    def handed(i, da, db):
        dx, dy = me.turn_other(jnp.int32(da), jnp.int32(db))
        x, y = block(dx, dy)
        wait(kv.at[i, others, x, y], s_recv.at[i, dx, dy])

    def along_b(i, k):
        for j, o in enumerate(RING):
            send(blk(i, COLS[k], 0), b_send.at[i, j, k], b_recv.at[i, j, k], me.at(a, (b + 4 - o) % 4))
        hand_over(i, COLS[k], 0)

    def arrived(i, k):
        for j, o in enumerate(RING):
            wait(blk(i, COLS[k], o), b_recv.at[i, j, k])
            hand_over(i, COLS[k], o)

    def handed_far(i, k):
        for o in RING:
            handed(i, COLS[k], o)

    def handed_near(i):
        for k in range(4):
            handed(i, COLS[k], 0)
        handed_far(i, 0)

    for i in (K, V):
        wait(blk(i, 0, 0), z_recv.at[i])
        for j, o in enumerate(RING):
            send(blk(i, 0, 0), a_send.at[i, j], a_recv.at[i, j], me.at((a + 4 - o) % 4, b))
        along_b(i, 0)
    qTf[...] = jnp.transpose(f32(q[...]))
    gTf[...] = jnp.transpose(f32(g[...]))
    for i in (K, V):
        for k in range(1, 4):
            wait(blk(i, COLS[k], 0), a_recv.at[i, k - 1])
            along_b(i, k)
    arrived(K, 0)
    handed_near(K)
    each(NEAR, scores)
    arrived(V, 0)
    top(m_near)
    over(NEAR, weights(m_near))
    arrived(K, 1)
    arrived(K, 2)
    handed_near(V)
    over(NEAR, values_in)
    lo = NEAR[0] * BLK
    for r in range(0, R, RB):
        acc_near[r:r + RB, :] = dot(p_buf[r:r + RB, lo:], vo[lo:, :])
    each(NEAR, value_dots)
    arrived(K, 3)
    handed_far(K, 1)
    handed_far(K, 2)
    each(range(5, 9), scores)
    arrived(V, 1)
    handed_far(K, 3)
    each(range(5), scores)
    arrived(V, 2)
    top(m_all)
    over(FAR, weights(m_all))
    arrived(V, 3)
    for k in range(1, 4):
        handed_far(V, k)
    over(FAR, values_in)
    each(FAR, value_dots)
    for r in range(0, R, RB):
        rows = slice(r, r + RB)
        f = jnp.exp2((m_near[rows, :] - m_all[rows, :]) * C2)
        m_near[rows, :] = f
        part = dot(p_buf[rows, :lo], vo[:lo, :])
        total = part[:, :128] + f * acc_near[rows, :128]
        rl = 1.0 / (part[:, 128:] + f * acc_near[rows, 128:])
        mixed = jnp.where(valid[rows, :], total * rl, 0.0)
        attv[rows, :] = mixed.astype(BF16)
        off[rows, :] = jnp.broadcast_to(jnp.sum(f32(g[rows, :]) * mixed, axis=1, keepdims=True), (RB, 128))
        m_all[rows, :] = rl
        rlT = jnp.transpose(rl)
        fT = jnp.transpose(f)
        qs = qTf[:, rows] * (rlT * ROOT)
        gs = gTf[:, rows] * rlT
        qT[0, :, rows] = qs.astype(BF16)
        qT[1, :, rows] = (qs * fT).astype(BF16)
        gT[0, :, rows] = gs.astype(BF16)
        gT[1, :, rows] = (gs * fT).astype(BF16)

    def part_sum(n):
        wait(sbuf.at[n], rs_recv.at[n])
        return f32(sbuf[n]) + f32(gbuf[n, :, mine])

    def to_b(n):
        if isinstance(n, int):
            da, db = me.turn(jnp.int32(STEPS[n][0]), jnp.int32(STEPS[n][1]))
        else:
            da, db = me.turn(pick(n, [s[0] for s in STEPS]), pick(n, [s[1] for s in STEPS]))

        @pl.when(db != 0)
        def _():
            sbuf[n] = part_sum(n).astype(BF16)
            rcopy(sbuf.at[n], bbuf.at[db - 1, da], rb_send.at[db - 1, da], rb_recv.at[db - 1, da],
                  me.at(a, (b + db) % 4)).start()

    def gradients(n, far):
        cols = at_pos(n)
        kg, vg = jnp.zeros((128, BLK), F32), jnp.zeros((128, BLK), F32)
        for r in range(0, R, RB):
            rows = slice(r, r + RB)
            p = p_buf[rows, cols]
            o = jnp.concatenate([off[rows, :]] * 2, axis=1)
            ds = (f32(p) * (vd_buf[n, rows, :] - o)).astype(BF16)
            p_buf[rows, cols] = ds
            kg += dot(qT[far, :, rows], ds)
            vg += dot(gT[far, :, rows], p)
        gbuf[n, K] = jnp.transpose(kg).astype(BF16).reshape(NZ, 32, 128)
        gbuf[n, V] = jnp.transpose(vg).astype(BF16).reshape(NZ, 32, 128)

    def to_sibling(n):
        rcopy(gbuf.at[n, :, others], sbuf.at[n], rs_send.at[n], rs_recv.at[n], sib).start()

    def three(i, _):
        for j in range(3):
            gradients(3 * i + j, 0)
        for j in range(3):
            to_sibling(3 * i + j)

        @pl.when(i > 0)
        def _():
            for j in range(3):
                to_b(3 * i + j - 3)
        return 0

    lax.fori_loop(0, 3, three, 0)
    for now, before in ((NEAR[:4], FAR[6:]), (NEAR[4:], NEAR[:4]), ((), (13, 14))):
        for n in now:
            gradients(n, 1)
        for n in now:
            to_sibling(n)
        for n in before:
            to_b(n)

    tail = []
    for n in NEAR:
        da, dy = STEPS[n]
        if da and not dy:
            m = n + c * (STEPS.index((0, da)) - n)
            total = part_sum(m)
            for j in range(3):
                wait(bbuf.at[j, da], rb_recv.at[j, da])
                total = total + f32(bbuf[j, da])
            sbuf[m] = total.astype(BF16)
            cp = rcopy(sbuf.at[m], abuf.at[da - 1], ra_send.at[da - 1], ra_recv.at[da - 1], me.at((a + da) % 4, b))
            cp.start()
            tail.append(cp)
    for r in range(0, R, RB):
        rows = slice(r, r + RB)
        t = dot(p_buf[rows, :lo], kord[:lo, :]) + m_near[rows, :] * dot(p_buf[rows, lo:], kord[lo:, :])
        qgv[rows, :] = (t * (m_all[rows, :] * ROOT)).astype(BF16)
    total = part_sum(15)
    for j in range(3):
        wait(bbuf.at[j, 0], rb_recv.at[j, 0])
        total = total + f32(bbuf[j, 0])
    for j in range(3):
        wait(abuf.at[j], ra_recv.at[j])
        total = total + f32(abuf[j])
    w[...] = total.astype(BF16)
    for d in (2, 1, 3, 0):
        t = lax.rem(z + d, 4)
        for r in range(2):
            ct = (c + r) % 2
            src, dst = w.at[:, t, pl.ds(pl.multiple_of(ct * 16, 16), 16)], zbuf.at[:, z]
            if d or r:
                rcopy(src, dst, rz_send, rz_recv, me.chip(c * 4 + t, ct)).start()
            else:
                to_or_keep(src, dst, rz_self, rz_recv, my_half == c, me.chip(c * 4 + t, ct))
    for cp in sends + tail:
        cp.wait_send()
    for i in (K, V):
        wait(sendbuf.at[i, pl.ds(0, 7)], z_send.at[i])

        @pl.when(my_half != c)
        def _():
            wait(sendbuf.at[i, 0], z_self.at[i])
    for n in range(16):
        wait(sbuf.at[n], rs_send.at[n])
    for j in range(3):
        for k in range(4):
            wait(bbuf.at[j, k], rb_send.at[j, k])
    wait(zbuf.at[:, pl.ds(0, 7)], rz_send)

    @pl.when(my_half != c)
    def _():
        wait(zbuf.at[:, 0], rz_self)
    wait(zbuf, rz_recv)


def write_kernel(att_in, qg_in, zbuf, att, qg, kg, vg, buf, sem):
    cps = [pltpu.make_async_copy(att_in, att, sem.at[0]), pltpu.make_async_copy(qg_in, qg, sem.at[1])]
    for cp in cps:
        cp.start()
    for i, dst in enumerate((kg, vg)):
        for h in range(NZ):
            buf[i, pl.ds(h, 16, stride=8), :] = f32(zbuf[i, h])
        cps.append(pltpu.make_async_copy(buf.at[i], dst, sem.at[2 + i]))
        cps[-1].start()
    for cp in cps:
        cp.wait()


def on_device(queries, prefix_keys, prefix_values, out_grad, tile_mask, lengths):
    R = queries.shape[0] * queries.shape[1]
    S = 16 * BLK
    sm, hbm = pl.BlockSpec(memory_space=pltpu.SMEM), pl.BlockSpec(memory_space=pl.ANY)
    vmem, dma = pltpu.VMEM, pltpu.SemaphoreType.DMA
    rows = jax.ShapeDtypeStruct((R, 128), BF16)
    att, qg, heads = pl.pallas_call(
        kernel,
        out_shape=(rows, rows, jax.ShapeDtypeStruct((2, NZ, 16, 128), BF16)),
        in_specs=[sm, sm, hbm, hbm, hbm, hbm],
        out_specs=(pl.BlockSpec(memory_space=vmem),) * 3,
        scratch_shapes=[
            vmem((16, 8, 128), BF16), vmem((16, 8, 128), BF16), vmem((R, 128), BF16), vmem((R, 128), BF16),
            vmem((2, 128, 128), F32), vmem((2, NZ, 16, 128), BF16), vmem((2, NZ, 4, 4, 32, 128), BF16),
            vmem((S, 256), BF16), vmem((S, 128), BF16), vmem((4, 8, BLK), F32),
            vmem((16, R, BLK), F32), vmem((16, R, BLK), F32), vmem((R, S), BF16),
            vmem((R, 128), F32), vmem((R, 128), F32), vmem((R, 128), F32),
            vmem((R, 128), F32), vmem((R, 256), F32),
            vmem((128, R), F32), vmem((128, R), F32), vmem((2, 128, R), BF16), vmem((2, 128, R), BF16),
            vmem((16, 2, NZ, 32, 128), BF16), vmem((16, 2, 4, 32, 128), BF16), vmem((3, 4, 2, 4, 32, 128), BF16),
            vmem((3, 2, 4, 32, 128), BF16), vmem((2, 4, 32, 128), BF16),
            dma((4,)), dma((2,)), dma((2,)), dma((2,)), dma((2, 3)), dma((2, 3)), dma((2, 3, 4)), dma((2, 3, 4)),
            dma((2, 4, 4)), dma((2, 4, 4)), dma((16,)), dma((16,)), dma((3, 4)), dma((3, 4)),
            dma((3,)), dma((3,)), dma, dma, dma,
        ],
        compiler_params=pltpu.CompilerParams(collective_id=0, has_side_effects=True,
                                             vmem_limit_bytes=60 * 2**20),
        name="shared_prompt",
    )(tile_mask, lengths, queries.reshape(R, 128), out_grad.reshape(R, 128), prefix_keys, prefix_values)
    grads = jax.ShapeDtypeStruct((128, 128), F32)
    att, qg, kg, vg = pl.pallas_call(
        write_kernel,
        out_shape=(rows, rows, grads, grads),
        in_specs=[pl.BlockSpec(memory_space=vmem)] * 3,
        out_specs=(hbm, hbm, hbm, hbm),
        scratch_shapes=[vmem((2, 128, 128), F32), dma((4,))],
        name="write_out",
    )(att, qg, heads)
    shape = prefix_keys.shape
    return att.reshape(queries.shape), qg.reshape(queries.shape), kg.reshape(shape), vg.reshape(shape)


def solution(mesh):
    tokens, owned = P("prefix", "group", None), P(("group", "prefix"), None, None)
    return jax.shard_map(
        on_device,
        mesh=mesh,
        in_specs=(tokens, owned, owned, tokens, P(), P()),
        out_specs=(tokens, tokens, owned, owned),
        check_vma=False,
    )
```

```python
import functools
import math

import jax
import jax.numpy as jnp
from jax import lax
from jax.experimental import pallas as pl
from jax.experimental.pallas import tpu as pltpu
from jax.sharding import PartitionSpec as P

F32, BF16 = jnp.float32, jnp.bfloat16
MESH = pl.DeviceIdType.MESH
NZ = 8
BLK = 256
SPAN = 2048
ROOT = 1.0 / math.sqrt(128)
C2 = ROOT * math.log2(math.e)
HIDDEN = -1e30

STEPS = [(2, 2), (2, 1), (1, 2), (2, 3), (3, 2), (1, 1), (1, 3), (3, 1), (3, 3),
         (2, 0), (0, 2), (1, 0), (0, 1), (3, 0), (0, 3), (0, 0)]
FAR, NEAR = range(0, 9), range(9, 16)
RING = (3, 1, 2)
COLS = (0, 3, 1, 2)


class Place:
    def __init__(self):
        self.z = lax.axis_index("group")
        p = lax.axis_index("prefix")
        self.x, self.y, self.c = p // 8, p // 2 % 4, p % 2
        self.a, self.b = self.turn(self.x, self.y)

    def turn(self, u, v):
        return u + self.c * (v - u), v + self.c * (u - v)

    def turn_other(self, u, v):
        return u + (1 - self.c) * (v - u), v + (1 - self.c) * (u - v)

    def at(self, a, b):
        x, y = self.turn(a, b)
        return (self.z, (x * 4 + y) * 2 + self.c)

    def chip(self, z, c):
        return (z, (self.x * 4 + self.y) * 2 + c)


def rcopy(src, dst, ss, rs, dev):
    return pltpu.make_async_remote_copy(src_ref=src, dst_ref=dst, send_sem=ss, recv_sem=rs,
                                        device_id=dev, device_id_type=MESH)


def wait(ref, sem):
    pltpu.make_async_copy(ref, ref, sem).wait()


def dot(u, v):
    return jnp.dot(u, v, preferred_element_type=F32)


def dot_nt(u, v):
    return lax.dot_general(u, v, (((1,), (1,)), ((), ())), preferred_element_type=F32)


def f32(v):
    return v.astype(F32)


def over(ns, body):
    ns = list(ns)
    straight = ns == list(range(ns[0], ns[0] + len(ns)))
    codes = (0 if straight else sum(n * 16**i for i, n in enumerate(ns)),
             sum(STEPS[n][0] * 4**i for i, n in enumerate(ns)),
             sum(STEPS[n][1] * 4**i for i, n in enumerate(ns)))

    def one(i, carry):
        cn, cx, cy = carry
        body(ns[0] + i if straight else lax.rem(cn, 16), lax.rem(cx, 4), lax.rem(cy, 4))
        return lax.div(cn, 16), lax.div(cx, 4), lax.div(cy, 4)

    lax.fori_loop(0, len(ns), one, tuple(jnp.int32(v) for v in codes))


def each(ns, body):
    for n in ns:
        body(n, *STEPS[n])


def pick(n, values):
    out = jnp.int32(values[0])
    for i, v in enumerate(values[1:], 1):
        out = jnp.where(n == i, v, out)
    return out


def kernel(mask_ref, len_ref, q_hbm, g_hbm, k_hbm, v_hbm, attv, qgv, zbuf,
           kin, vin, q, g, strips, sendbuf, kv, vo, kord, bias, s_buf, vd_buf, p_buf, m_part, m_near, m_all,
           off, acc_near, qTf, gTf, qT, gT, gbuf, sbuf, bbuf, abuf, w,
           in_sem, z_send, z_self, z_recv, a_send, a_recv, b_send, b_recv, s_send, s_recv,
           rs_send, rs_recv, rb_send, rb_recv, ra_send, ra_recv, rz_send, rz_self, rz_recv):
    me = Place()
    a, b, z, c = me.a, me.b, me.z, me.c
    R = q.shape[0]
    RB = 256
    K, V = 0, 1
    sib = me.chip(z, 1 - c)
    mine, others = pl.ds(pl.multiple_of(c * 4, 4), 4), pl.ds(pl.multiple_of(4 - c * 4, 4), 4)
    my_half = lax.div(z, 4)
    ins = [pltpu.make_async_copy(s, d, in_sem.at[i])
           for i, (s, d) in enumerate(((k_hbm, kin), (v_hbm, vin), (q_hbm, q), (g_hbm, g)))]
    for cp in ins:
        cp.start()
    barrier = pltpu.get_barrier_semaphore()
    partners = [me.at((a + o) % 4, b) for o in (1, 2, 3)] + [me.at(a, (b + o) % 4) for o in (1, 2, 3)]
    partners += [me.chip((z + d) % NZ, (c + r) % 2) for d in range(NZ) for r in range(2) if d or r]
    for dev in partners:
        pl.semaphore_signal(barrier, inc=1, device_id=dev, device_id_type=MESH)
    for i, ref in enumerate((kin, vin)):
        ins[i].wait()
        strips[i] = f32(ref[...]).reshape(128, 128)
        for h in range(NZ):
            sendbuf[i, h] = strips[i, pl.ds(h, 16, stride=8), :].astype(BF16)
    pl.semaphore_wait(barrier, len(partners))

    def to_or_keep(src, dst, ss, rs, here, dev):
        @pl.when(here)
        def _():
            pltpu.make_async_copy(src, dst, rs).start()

        @pl.when(jnp.logical_not(here))
        def _():
            rcopy(src, dst, ss, rs, dev).start()

    strip = pl.ds(pl.multiple_of(c * 16, 16), 16)
    for i in (K, V):
        dst = kv.at[i, me.x, me.y, z, strip]
        for d in (4, 3, 5, 2, 6, 1, 7):
            h = (z + d) % NZ
            rcopy(sendbuf.at[i, h], dst, z_send.at[i], z_recv.at[i], me.chip(h, my_half)).start()
        to_or_keep(sendbuf.at[i, z], dst, z_self.at[i], z_recv.at[i], my_half == c, sib)

    ins[2].wait()
    ins[3].wait()
    comp = lax.axis_index("prefix") * (R // 8) // SPAN
    nrow = (len_ref[comp] - lax.axis_index("prefix") * (R // 8) % SPAN) * 8
    valid = lax.broadcasted_iota(jnp.int32, (R, 128), 0) < nrow
    g[...] = jnp.where(valid, f32(g[...]), 0.0).astype(BF16)
    vo[:, 128:256] = jnp.ones((vo.shape[0], 128), BF16)
    lane = lax.broadcasted_iota(jnp.int32, (8, BLK), 1) // 32
    for x in range(4):
        row = jnp.zeros((8, BLK), F32)
        for zz in range(NZ):
            t = zz * 4 + x
            if t:
                level = (1.0 - mask_ref[comp, t].astype(F32)) * HIDDEN
                row = jnp.where(lane == zz, level, row)
        bias[x] = row
    m_part[...] = jnp.full((R, 128), -jnp.inf, F32)

    def block(dx, dy):
        return (me.x + dx) % 4, (me.y + dy) % 4

    def at_pos(n):
        return pl.ds(n * BLK if isinstance(n, int) else pl.multiple_of(n * BLK, BLK), BLK)

    def scores(n, dx, dy):
        x, y = block(dx, dy)
        k = kv[K, x, y].reshape(BLK, 128)
        kord[at_pos(n), :] = k
        for r in range(0, R, RB):
            s = dot_nt(q[r:r + RB, :], k)
            s = (s.reshape(RB // 8, 8, BLK) + bias[x][None]).reshape(RB, BLK)
            s_buf[n, r:r + RB, :] = s
            m_part[r:r + RB, :] = jnp.maximum(m_part[r:r + RB, :], jnp.maximum(s[:, :128], s[:, 128:]))

    def values_in(n, dx, dy):
        x, y = block(dx, dy)
        vo[at_pos(n), 0:128] = kv[V, x, y].reshape(BLK, 128)

    def value_dots(n, dx, dy):
        v = vo[at_pos(n), 0:128]
        for r in range(0, R, RB):
            vd_buf[n, r:r + RB, :] = dot_nt(g[r:r + RB, :], v)

    def weights(m_ref):
        def one(n, dx, dy):
            for r in range(0, R, RB):
                m = m_ref[r:r + RB, :]
                for j in range(2):
                    p = jnp.exp2((s_buf[n, r:r + RB, 128 * j:128 * j + 128] - m) * C2)
                    p_buf[r:r + RB, pl.ds(pl.multiple_of(n * BLK + 128 * j, 128), 128)] = p.astype(BF16)
        return one

    def top(ref):
        ref[...] = jnp.broadcast_to(jnp.max(m_part[...], axis=1, keepdims=True), (R, 128))

    sends = []

    def send(ref, ss, rs, dev):
        cp = rcopy(ref, ref, ss, rs, dev)
        cp.start()
        sends.append(cp)

    def blk(i, da, db):
        x, y = me.turn((a + da) % 4, (b + db) % 4)
        return kv.at[i, x, y, mine]

    def hand_over(i, da, db):
        dx, dy = me.turn(jnp.int32(da), jnp.int32(db))
        send(blk(i, da, db), s_send.at[i, da, db], s_recv.at[i, dx, dy], sib)

    def handed(i, da, db):
        dx, dy = me.turn_other(jnp.int32(da), jnp.int32(db))
        x, y = block(dx, dy)
        wait(kv.at[i, x, y, others], s_recv.at[i, dx, dy])

    def along_b(i, k):
        for j, o in ((2, 2), (0, 3), (1, 1)):
            send(blk(i, COLS[k], 0), b_send.at[i, j, k], b_recv.at[i, j, k], me.at(a, (b + 4 - o) % 4))
        hand_over(i, COLS[k], 0)

    def arrived(i, k):
        for j, o in enumerate(RING):
            wait(blk(i, COLS[k], o), b_recv.at[i, j, k])
            hand_over(i, COLS[k], o)

    def handed_far(i, k):
        for o in RING:
            handed(i, COLS[k], o)

    def handed_near(i):
        for k in range(4):
            handed(i, COLS[k], 0)
        handed_far(i, 0)

    for i in (K, V):
        wait(blk(i, 0, 0), z_recv.at[i])
        for j, o in ((2, 2), (0, 3), (1, 1)):
            send(blk(i, 0, 0), a_send.at[i, j], a_recv.at[i, j], me.at((a + 4 - o) % 4, b))
        along_b(i, 0)
    qTf[...] = jnp.transpose(f32(q[...]))
    gTf[...] = jnp.transpose(f32(g[...]))
    for i in (K, V):
        for k in range(1, 4):
            wait(blk(i, COLS[k], 0), a_recv.at[i, k - 1])
            along_b(i, k)
    arrived(K, 0)
    handed_near(K)
    each(NEAR, scores)
    arrived(V, 0)
    top(m_near)
    over(NEAR, weights(m_near))
    arrived(K, 1)
    arrived(K, 2)
    handed_near(V)
    over(NEAR, values_in)
    lo = NEAR[0] * BLK
    for r in range(0, R, RB):
        acc_near[r:r + RB, :] = dot(p_buf[r:r + RB, lo:], vo[lo:, :])
    each(NEAR, value_dots)
    arrived(K, 3)
    handed_far(K, 1)
    handed_far(K, 2)
    each(range(5, 9), scores)
    handed_far(K, 3)
    each(range(5), scores)
    top(m_all)
    arrived(V, 1)
    over(range(5), weights(m_all))
    arrived(V, 2)
    over(range(5, 9), weights(m_all))
    arrived(V, 3)
    handed_far(V, 1)
    handed_far(V, 2)
    over(range(5, 9), values_in)
    each(range(5, 9), value_dots)
    handed_far(V, 3)
    over(range(5), values_in)
    each(range(5), value_dots)
    for r in range(0, R, RB):
        rows = slice(r, r + RB)
        f = jnp.exp2((m_near[rows, :] - m_all[rows, :]) * C2)
        m_near[rows, :] = f
        part = dot(p_buf[rows, :lo], vo[:lo, :])
        total = part[:, :128] + f * acc_near[rows, :128]
        rl = 1.0 / (part[:, 128:] + f * acc_near[rows, 128:])
        mixed = jnp.where(valid[rows, :], total * rl, 0.0)
        attv[rows, :] = mixed.astype(BF16)
        off[rows, :] = jnp.broadcast_to(jnp.sum(f32(g[rows, :]) * mixed, axis=1, keepdims=True), (RB, 128))
        m_all[rows, :] = rl
        rlT = jnp.transpose(rl)
        fT = jnp.transpose(f)
        qs = qTf[:, rows] * (rlT * ROOT)
        gs = gTf[:, rows] * rlT
        qT[0, :, rows] = qs.astype(BF16)
        qT[1, :, rows] = (qs * fT).astype(BF16)
        gT[0, :, rows] = gs.astype(BF16)
        gT[1, :, rows] = (gs * fT).astype(BF16)

    def part_sum(n):
        wait(sbuf.at[n], rs_recv.at[n])
        return f32(sbuf[n]) + f32(gbuf[n, :, mine])

    def to_b(n):
        if isinstance(n, int):
            da, db = me.turn(jnp.int32(STEPS[n][0]), jnp.int32(STEPS[n][1]))
        else:
            da, db = me.turn(pick(n, [s[0] for s in STEPS]), pick(n, [s[1] for s in STEPS]))

        @pl.when(db != 0)
        def _():
            sbuf[n] = part_sum(n).astype(BF16)
            rcopy(sbuf.at[n], bbuf.at[db - 1, da], rb_send.at[db - 1, da], rb_recv.at[db - 1, da],
                  me.at(a, (b + db) % 4)).start()

    def gradients(n, far):
        cols = at_pos(n)
        kg, vg = jnp.zeros((128, BLK), F32), jnp.zeros((128, BLK), F32)
        for r in range(0, R, RB):
            rows = slice(r, r + RB)
            p = p_buf[rows, cols]
            o = jnp.concatenate([off[rows, :]] * 2, axis=1)
            ds = (f32(p) * (vd_buf[n, rows, :] - o)).astype(BF16)
            p_buf[rows, cols] = ds
            kg += dot(qT[far, :, rows], ds)
            vg += dot(gT[far, :, rows], p)
        gbuf[n, K] = jnp.transpose(kg).astype(BF16).reshape(NZ, 32, 128)
        gbuf[n, V] = jnp.transpose(vg).astype(BF16).reshape(NZ, 32, 128)

    def to_sibling(n):
        rcopy(gbuf.at[n, :, others], sbuf.at[n], rs_send.at[n], rs_recv.at[n], sib).start()

    def three(i, _):
        for j in range(3):
            gradients(3 * i + j, 0)
        for j in range(3):
            to_sibling(3 * i + j)

        @pl.when(i > 0)
        def _():
            for j in range(3):
                to_b(3 * i + j - 3)
        return 0

    lax.fori_loop(0, 3, three, 0)
    for now, before in ((NEAR[:4], FAR[6:]), (NEAR[4:], NEAR[:4]), ((), (13, 14))):
        for n in now:
            gradients(n, 1)
        for n in now:
            to_sibling(n)
        for n in before:
            to_b(n)

    tail = []
    for n in NEAR:
        da, dy = STEPS[n]
        if da and not dy:
            m = n + c * (STEPS.index((0, da)) - n)
            total = part_sum(m)
            for j in range(3):
                wait(bbuf.at[j, da], rb_recv.at[j, da])
                total = total + f32(bbuf[j, da])
            sbuf[m] = total.astype(BF16)
            cp = rcopy(sbuf.at[m], abuf.at[da - 1], ra_send.at[da - 1], ra_recv.at[da - 1], me.at((a + da) % 4, b))
            cp.start()
            tail.append(cp)
    for r in range(0, R, RB):
        rows = slice(r, r + RB)
        t = dot(p_buf[rows, :lo], kord[:lo, :]) + m_near[rows, :] * dot(p_buf[rows, lo:], kord[lo:, :])
        qgv[rows, :] = (t * (m_all[rows, :] * ROOT)).astype(BF16)
    total = part_sum(15)
    for j in range(3):
        wait(bbuf.at[j, 0], rb_recv.at[j, 0])
        total = total + f32(bbuf[j, 0])
    for j in range(3):
        wait(abuf.at[j], ra_recv.at[j])
        total = total + f32(abuf[j])
    w[...] = total.astype(BF16)
    for d in (2, 1, 3, 0):
        t = lax.rem(z + d, 4)
        for r in range(2):
            ct = (c + r) % 2
            src, dst = w.at[:, t, pl.ds(pl.multiple_of(ct * 16, 16), 16)], zbuf.at[:, z]
            if d or r:
                rcopy(src, dst, rz_send, rz_recv, me.chip(c * 4 + t, ct)).start()
            else:
                to_or_keep(src, dst, rz_self, rz_recv, my_half == c, me.chip(c * 4 + t, ct))
    for cp in sends + tail:
        cp.wait_send()
    for i in (K, V):
        wait(sendbuf.at[i, pl.ds(0, 7)], z_send.at[i])

        @pl.when(my_half != c)
        def _():
            wait(sendbuf.at[i, 0], z_self.at[i])
    for n in range(16):
        wait(sbuf.at[n], rs_send.at[n])
    for j in range(3):
        for k in range(4):
            wait(bbuf.at[j, k], rb_send.at[j, k])
    wait(zbuf.at[:, pl.ds(0, 7)], rz_send)

    @pl.when(my_half != c)
    def _():
        wait(zbuf.at[:, 0], rz_self)
    wait(zbuf, rz_recv)


def write_kernel(att_in, qg_in, zbuf, att, qg, kg, vg, buf, sem):
    cps = [pltpu.make_async_copy(att_in, att, sem.at[0]), pltpu.make_async_copy(qg_in, qg, sem.at[1])]
    for cp in cps:
        cp.start()
    for i, dst in enumerate((kg, vg)):
        for h in range(NZ):
            buf[i, pl.ds(h, 16, stride=8), :] = f32(zbuf[i, h])
        cps.append(pltpu.make_async_copy(buf.at[i], dst, sem.at[2 + i]))
        cps[-1].start()
    for cp in cps:
        cp.wait()


def on_device(queries, prefix_keys, prefix_values, out_grad, tile_mask, lengths):
    R = queries.shape[0] * queries.shape[1]
    S = 16 * BLK
    sm, hbm = pl.BlockSpec(memory_space=pltpu.SMEM), pl.BlockSpec(memory_space=pl.ANY)
    vmem, dma = pltpu.VMEM, pltpu.SemaphoreType.DMA
    rows = jax.ShapeDtypeStruct((R, 128), BF16)
    att, qg, heads = pl.pallas_call(
        kernel,
        out_shape=(rows, rows, jax.ShapeDtypeStruct((2, NZ, 16, 128), BF16)),
        in_specs=[sm, sm, hbm, hbm, hbm, hbm],
        out_specs=(pl.BlockSpec(memory_space=vmem),) * 3,
        scratch_shapes=[
            vmem((16, 8, 128), BF16), vmem((16, 8, 128), BF16), vmem((R, 128), BF16), vmem((R, 128), BF16),
            vmem((2, 128, 128), F32), vmem((2, NZ, 16, 128), BF16), vmem((2, 4, 4, NZ, 32, 128), BF16),
            vmem((S, 256), BF16), vmem((S, 128), BF16), vmem((4, 8, BLK), F32),
            vmem((16, R, BLK), F32), vmem((16, R, BLK), F32), vmem((R, S), BF16),
            vmem((R, 128), F32), vmem((R, 128), F32), vmem((R, 128), F32),
            vmem((R, 128), F32), vmem((R, 256), F32),
            vmem((128, R), F32), vmem((128, R), F32), vmem((2, 128, R), BF16), vmem((2, 128, R), BF16),
            vmem((16, 2, NZ, 32, 128), BF16), vmem((16, 2, 4, 32, 128), BF16), vmem((3, 4, 2, 4, 32, 128), BF16),
            vmem((3, 2, 4, 32, 128), BF16), vmem((2, 4, 32, 128), BF16),
            dma((4,)), dma((2,)), dma((2,)), dma((2,)), dma((2, 3)), dma((2, 3)), dma((2, 3, 4)), dma((2, 3, 4)),
            dma((2, 4, 4)), dma((2, 4, 4)), dma((16,)), dma((16,)), dma((3, 4)), dma((3, 4)),
            dma((3,)), dma((3,)), dma, dma, dma,
        ],
        compiler_params=pltpu.CompilerParams(collective_id=0, has_side_effects=True,
                                             vmem_limit_bytes=60 * 2**20),
        name="shared_prompt",
    )(tile_mask, lengths, queries.reshape(R, 128), out_grad.reshape(R, 128), prefix_keys, prefix_values)
    grads = jax.ShapeDtypeStruct((128, 128), F32)
    att, qg, kg, vg = pl.pallas_call(
        write_kernel,
        out_shape=(rows, rows, grads, grads),
        in_specs=[pl.BlockSpec(memory_space=vmem)] * 3,
        out_specs=(hbm, hbm, hbm, hbm),
        scratch_shapes=[vmem((2, 128, 128), F32), dma((4,))],
        name="write_out",
    )(att, qg, heads)
    shape = prefix_keys.shape
    return att.reshape(queries.shape), qg.reshape(queries.shape), kg.reshape(shape), vg.reshape(shape)


def solution(mesh):
    tokens, owned = P("prefix", "group", None), P(("group", "prefix"), None, None)
    return jax.shard_map(
        on_device,
        mesh=mesh,
        in_specs=(tokens, owned, owned, tokens, P(), P()),
        out_specs=(tokens, tokens, owned, owned),
        check_vma=False,
    )
```

```python
import functools
import math

import jax
import jax.numpy as jnp
from jax import lax
from jax.experimental import pallas as pl
from jax.experimental.pallas import tpu as pltpu
from jax.sharding import PartitionSpec as P

F32, BF16 = jnp.float32, jnp.bfloat16
MESH = pl.DeviceIdType.MESH
NZ = 8
BLK = 256
SPAN = 2048
ROOT = 1.0 / math.sqrt(128)
C2 = ROOT * math.log2(math.e)
HIDDEN = -1e30

STEPS = [(2, 2), (2, 1), (1, 2), (2, 3), (3, 2), (1, 1), (1, 3), (3, 1), (3, 3),
         (2, 0), (0, 2), (1, 0), (0, 1), (3, 0), (0, 3), (0, 0)]
FAR, NEAR = range(0, 9), range(9, 16)
RING = (3, 1, 2)
COLS = (0, 3, 1, 2)


class Place:
    def __init__(self):
        self.z = lax.axis_index("group")
        p = lax.axis_index("prefix")
        self.x, self.y, self.c = p // 8, p // 2 % 4, p % 2
        self.a, self.b = self.turn(self.x, self.y)

    def turn(self, u, v):
        return u + self.c * (v - u), v + self.c * (u - v)

    def turn_other(self, u, v):
        return u + (1 - self.c) * (v - u), v + (1 - self.c) * (u - v)

    def at(self, a, b):
        x, y = self.turn(a, b)
        return (self.z, (x * 4 + y) * 2 + self.c)

    def chip(self, z, c):
        return (z, (self.x * 4 + self.y) * 2 + c)


def rcopy(src, dst, ss, rs, dev):
    return pltpu.make_async_remote_copy(src_ref=src, dst_ref=dst, send_sem=ss, recv_sem=rs,
                                        device_id=dev, device_id_type=MESH)


def wait(ref, sem):
    pltpu.make_async_copy(ref, ref, sem).wait()


def dot(u, v):
    return jnp.dot(u, v, preferred_element_type=F32)


def dot_nt(u, v):
    return lax.dot_general(u, v, (((1,), (1,)), ((), ())), preferred_element_type=F32)


def f32(v):
    return v.astype(F32)


def over(ns, body):
    ns = list(ns)
    straight = ns == list(range(ns[0], ns[0] + len(ns)))
    codes = (0 if straight else sum(n * 16**i for i, n in enumerate(ns)),
             sum(STEPS[n][0] * 4**i for i, n in enumerate(ns)),
             sum(STEPS[n][1] * 4**i for i, n in enumerate(ns)))

    def one(i, carry):
        cn, cx, cy = carry
        body(ns[0] + i if straight else lax.rem(cn, 16), lax.rem(cx, 4), lax.rem(cy, 4))
        return lax.div(cn, 16), lax.div(cx, 4), lax.div(cy, 4)

    lax.fori_loop(0, len(ns), one, tuple(jnp.int32(v) for v in codes))


def each(ns, body):
    for n in ns:
        body(n, *STEPS[n])


def pick(n, values):
    out = jnp.int32(values[0])
    for i, v in enumerate(values[1:], 1):
        out = jnp.where(n == i, v, out)
    return out


def kernel(mask_ref, len_ref, q_hbm, g_hbm, k_hbm, v_hbm, att_hbm, qg_hbm, zbuf,
           attv, qgv, out_sem, kin, vin, q, g, strips, sendbuf, kv, vo, kord, bias, s_buf, vd_buf, p_buf, m_part, m_near, m_all,
           off, acc_near, qTf, gTf, qT, gT, gbuf, sbuf, bbuf, abuf, w,
           in_sem, z_send, z_self, z_recv, a_send, a_recv, b_send, b_recv, s_send, s_recv,
           rs_send, rs_recv, rb_send, rb_recv, ra_send, ra_recv, rz_send, rz_self, rz_recv):
    me = Place()
    a, b, z, c = me.a, me.b, me.z, me.c
    R = q.shape[0]
    RB = 256
    K, V = 0, 1
    sib = me.chip(z, 1 - c)
    mine, others = pl.ds(pl.multiple_of(c * 4, 4), 4), pl.ds(pl.multiple_of(4 - c * 4, 4), 4)
    my_half = lax.div(z, 4)
    ins = [pltpu.make_async_copy(s, d, in_sem.at[i])
           for i, (s, d) in enumerate(((k_hbm, kin), (v_hbm, vin), (q_hbm, q), (g_hbm, g)))]
    for cp in ins:
        cp.start()
    barrier = pltpu.get_barrier_semaphore()
    partners = [me.at((a + o) % 4, b) for o in (1, 2, 3)] + [me.at(a, (b + o) % 4) for o in (1, 2, 3)]
    partners += [me.chip((z + d) % NZ, (c + r) % 2) for d in range(NZ) for r in range(2) if d or r]
    for dev in partners:
        pl.semaphore_signal(barrier, inc=1, device_id=dev, device_id_type=MESH)
    for i, ref in enumerate((kin, vin)):
        ins[i].wait()
        strips[i] = f32(ref[...]).reshape(128, 128)
        for h in range(NZ):
            sendbuf[i, h] = strips[i, pl.ds(h, 16, stride=8), :].astype(BF16)
    pl.semaphore_wait(barrier, len(partners))

    def to_or_keep(src, dst, ss, rs, here, dev):
        @pl.when(here)
        def _():
            pltpu.make_async_copy(src, dst, rs).start()

        @pl.when(jnp.logical_not(here))
        def _():
            rcopy(src, dst, ss, rs, dev).start()

    strip = pl.ds(pl.multiple_of(c * 16, 16), 16)
    for i in (K, V):
        dst = kv.at[i, me.x, me.y, z, strip]
        for d in (4, 3, 5, 2, 6, 1, 7):
            h = (z + d) % NZ
            rcopy(sendbuf.at[i, h], dst, z_send.at[i], z_recv.at[i], me.chip(h, my_half)).start()
        to_or_keep(sendbuf.at[i, z], dst, z_self.at[i], z_recv.at[i], my_half == c, sib)

    ins[2].wait()
    ins[3].wait()
    comp = lax.axis_index("prefix") * (R // 8) // SPAN
    nrow = (len_ref[comp] - lax.axis_index("prefix") * (R // 8) % SPAN) * 8
    valid = lax.broadcasted_iota(jnp.int32, (R, 128), 0) < nrow
    g[...] = jnp.where(valid, f32(g[...]), 0.0).astype(BF16)
    vo[:, 128:256] = jnp.ones((vo.shape[0], 128), BF16)
    lane = lax.broadcasted_iota(jnp.int32, (8, BLK), 1) // 32
    for x in range(4):
        row = jnp.zeros((8, BLK), F32)
        for zz in range(NZ):
            t = zz * 4 + x
            if t:
                level = (1.0 - mask_ref[comp, t].astype(F32)) * HIDDEN
                row = jnp.where(lane == zz, level, row)
        bias[x] = row
    m_part[...] = jnp.full((R, 128), -jnp.inf, F32)

    def block(dx, dy):
        return (me.x + dx) % 4, (me.y + dy) % 4

    def at_pos(n):
        return pl.ds(n * BLK if isinstance(n, int) else pl.multiple_of(n * BLK, BLK), BLK)

    def scores(n, dx, dy):
        x, y = block(dx, dy)
        k = kv[K, x, y].reshape(BLK, 128)
        kord[at_pos(n), :] = k
        for r in range(0, R, RB):
            s = dot_nt(q[r:r + RB, :], k)
            s = (s.reshape(RB // 8, 8, BLK) + bias[x][None]).reshape(RB, BLK)
            s_buf[n, r:r + RB, :] = s
            m_part[r:r + RB, :] = jnp.maximum(m_part[r:r + RB, :], jnp.maximum(s[:, :128], s[:, 128:]))

    def values_in(n, dx, dy):
        x, y = block(dx, dy)
        vo[at_pos(n), 0:128] = kv[V, x, y].reshape(BLK, 128)

    def value_dots(n, dx, dy):
        v = vo[at_pos(n), 0:128]
        for r in range(0, R, RB):
            vd_buf[n, r:r + RB, :] = dot_nt(g[r:r + RB, :], v)

    def weights(m_ref):
        def one(n, dx, dy):
            for r in range(0, R, RB):
                m = m_ref[r:r + RB, :]
                for j in range(2):
                    p = jnp.exp2((s_buf[n, r:r + RB, 128 * j:128 * j + 128] - m) * C2)
                    p_buf[r:r + RB, pl.ds(pl.multiple_of(n * BLK + 128 * j, 128), 128)] = p.astype(BF16)
        return one

    def top(ref):
        ref[...] = jnp.broadcast_to(jnp.max(m_part[...], axis=1, keepdims=True), (R, 128))

    sends = []

    def send(ref, ss, rs, dev):
        cp = rcopy(ref, ref, ss, rs, dev)
        cp.start()
        sends.append(cp)

    def blk(i, da, db):
        x, y = me.turn((a + da) % 4, (b + db) % 4)
        return kv.at[i, x, y, mine]

    def hand_over(i, da, db):
        dx, dy = me.turn(jnp.int32(da), jnp.int32(db))
        send(blk(i, da, db), s_send.at[i, da, db], s_recv.at[i, dx, dy], sib)

    def handed(i, da, db):
        dx, dy = me.turn_other(jnp.int32(da), jnp.int32(db))
        x, y = block(dx, dy)
        wait(kv.at[i, x, y, others], s_recv.at[i, dx, dy])

    def along_b(i, k):
        for j, o in ((2, 2), (0, 3), (1, 1)):
            send(blk(i, COLS[k], 0), b_send.at[i, j, k], b_recv.at[i, j, k], me.at(a, (b + 4 - o) % 4))
        hand_over(i, COLS[k], 0)

    def arrived(i, k):
        for j, o in enumerate(RING):
            wait(blk(i, COLS[k], o), b_recv.at[i, j, k])
            hand_over(i, COLS[k], o)

    def handed_far(i, k):
        for o in RING:
            handed(i, COLS[k], o)

    def handed_near(i):
        for k in range(4):
            handed(i, COLS[k], 0)
        handed_far(i, 0)

    for i in (K, V):
        wait(blk(i, 0, 0), z_recv.at[i])
        for j, o in ((2, 2), (0, 3), (1, 1)):
            send(blk(i, 0, 0), a_send.at[i, j], a_recv.at[i, j], me.at((a + 4 - o) % 4, b))
        along_b(i, 0)
    qTf[...] = jnp.transpose(f32(q[...]))
    gTf[...] = jnp.transpose(f32(g[...]))
    for i in (K, V):
        for k in range(1, 4):
            wait(blk(i, COLS[k], 0), a_recv.at[i, k - 1])
            along_b(i, k)
    arrived(K, 0)
    handed_near(K)
    each(NEAR, scores)
    arrived(V, 0)
    top(m_near)
    over(NEAR, weights(m_near))
    arrived(K, 1)
    arrived(K, 2)
    handed_near(V)
    over(NEAR, values_in)
    lo = NEAR[0] * BLK
    for r in range(0, R, RB):
        acc_near[r:r + RB, :] = dot(p_buf[r:r + RB, lo:], vo[lo:, :])
    each(NEAR, value_dots)
    arrived(K, 3)
    handed_far(K, 1)
    handed_far(K, 2)
    each(range(5, 9), scores)
    handed_far(K, 3)
    each(range(5), scores)
    top(m_all)
    arrived(V, 1)
    over(range(5), weights(m_all))
    arrived(V, 2)
    over(range(5, 9), weights(m_all))
    arrived(V, 3)
    handed_far(V, 1)
    handed_far(V, 2)
    over(range(5, 9), values_in)
    each(range(5, 9), value_dots)
    handed_far(V, 3)
    over(range(5), values_in)
    each(range(3), value_dots)
    for r in range(0, R, RB):
        rows = slice(r, r + RB)
        f = jnp.exp2((m_near[rows, :] - m_all[rows, :]) * C2)
        m_near[rows, :] = f
        part = dot(p_buf[rows, :lo], vo[:lo, :])
        total = part[:, :128] + f * acc_near[rows, :128]
        rl = 1.0 / (part[:, 128:] + f * acc_near[rows, 128:])
        mixed = jnp.where(valid[rows, :], total * rl, 0.0)
        attv[rows, :] = mixed.astype(BF16)
        off[rows, :] = jnp.broadcast_to(jnp.sum(f32(g[rows, :]) * mixed, axis=1, keepdims=True), (RB, 128))
        m_all[rows, :] = rl
        rlT = jnp.transpose(rl)
        fT = jnp.transpose(f)
        qs = qTf[:, rows] * (rlT * ROOT)
        gs = gTf[:, rows] * rlT
        qT[0, :, rows] = qs.astype(BF16)
        qT[1, :, rows] = (qs * fT).astype(BF16)
        gT[0, :, rows] = gs.astype(BF16)
        gT[1, :, rows] = (gs * fT).astype(BF16)

    att_out = pltpu.make_async_copy(attv, att_hbm, out_sem.at[0])
    att_out.start()

    def part_sum(n):
        wait(sbuf.at[n], rs_recv.at[n])
        return f32(sbuf[n]) + f32(gbuf[n, :, mine])

    def to_b(n):
        if isinstance(n, int):
            da, db = me.turn(jnp.int32(STEPS[n][0]), jnp.int32(STEPS[n][1]))
        else:
            da, db = me.turn(pick(n, [s[0] for s in STEPS]), pick(n, [s[1] for s in STEPS]))

        @pl.when(db != 0)
        def _():
            sbuf[n] = part_sum(n).astype(BF16)
            rcopy(sbuf.at[n], bbuf.at[db - 1, da], rb_send.at[db - 1, da], rb_recv.at[db - 1, da],
                  me.at(a, (b + db) % 4)).start()

    def gradients(n, far):
        cols = at_pos(n)
        kg, vg = jnp.zeros((128, BLK), F32), jnp.zeros((128, BLK), F32)
        for r in range(0, R, RB):
            rows = slice(r, r + RB)
            p = p_buf[rows, cols]
            o = jnp.concatenate([off[rows, :]] * 2, axis=1)
            ds = (f32(p) * (vd_buf[n, rows, :] - o)).astype(BF16)
            p_buf[rows, cols] = ds
            kg += dot(qT[far, :, rows], ds)
            vg += dot(gT[far, :, rows], p)
        gbuf[n, K] = jnp.transpose(kg).astype(BF16).reshape(NZ, 32, 128)
        gbuf[n, V] = jnp.transpose(vg).astype(BF16).reshape(NZ, 32, 128)

    def to_sibling(n):
        rcopy(gbuf.at[n, :, others], sbuf.at[n], rs_send.at[n], rs_recv.at[n], sib).start()

    def three(i, _):
        for j in range(3):
            gradients(3 * i + j, 0)
        for j in range(3):
            to_sibling(3 * i + j)

        @pl.when(i == 0)
        def _():
            each((3, 4), value_dots)

        @pl.when(i > 0)
        def _():
            for j in range(3):
                to_b(3 * i + j - 3)
        return 0

    lax.fori_loop(0, 3, three, 0)
    for now, before in ((NEAR[:4], FAR[6:]), (NEAR[4:], NEAR[:4]), ((), (13, 14))):
        for n in now:
            gradients(n, 1)
        for n in now:
            to_sibling(n)
        for n in before:
            to_b(n)

    tail = []
    for n in NEAR:
        da, dy = STEPS[n]
        if da and not dy:
            m = n + c * (STEPS.index((0, da)) - n)
            total = part_sum(m)
            for j in range(3):
                wait(bbuf.at[j, da], rb_recv.at[j, da])
                total = total + f32(bbuf[j, da])
            sbuf[m] = total.astype(BF16)
            cp = rcopy(sbuf.at[m], abuf.at[da - 1], ra_send.at[da - 1], ra_recv.at[da - 1], me.at((a + da) % 4, b))
            cp.start()
            tail.append(cp)
    for r in range(0, R, RB):
        rows = slice(r, r + RB)
        t = dot(p_buf[rows, :lo], kord[:lo, :]) + m_near[rows, :] * dot(p_buf[rows, lo:], kord[lo:, :])
        qgv[rows, :] = (t * (m_all[rows, :] * ROOT)).astype(BF16)
    qg_out = pltpu.make_async_copy(qgv, qg_hbm, out_sem.at[1])
    qg_out.start()
    total = part_sum(15)
    for j in range(3):
        wait(bbuf.at[j, 0], rb_recv.at[j, 0])
        total = total + f32(bbuf[j, 0])
    for j in range(3):
        wait(abuf.at[j], ra_recv.at[j])
        total = total + f32(abuf[j])
    w[...] = total.astype(BF16)
    for d in (2, 1, 3, 0):
        t = lax.rem(z + d, 4)
        for r in range(2):
            ct = (c + r) % 2
            src, dst = w.at[:, t, pl.ds(pl.multiple_of(ct * 16, 16), 16)], zbuf.at[:, z]
            if d or r:
                rcopy(src, dst, rz_send, rz_recv, me.chip(c * 4 + t, ct)).start()
            else:
                to_or_keep(src, dst, rz_self, rz_recv, my_half == c, me.chip(c * 4 + t, ct))
    for cp in sends + tail:
        cp.wait_send()
    for i in (K, V):
        wait(sendbuf.at[i, pl.ds(0, 7)], z_send.at[i])

        @pl.when(my_half != c)
        def _():
            wait(sendbuf.at[i, 0], z_self.at[i])
    for n in range(16):
        wait(sbuf.at[n], rs_send.at[n])
    for j in range(3):
        for k in range(4):
            wait(bbuf.at[j, k], rb_send.at[j, k])
    wait(zbuf.at[:, pl.ds(0, 7)], rz_send)

    @pl.when(my_half != c)
    def _():
        wait(zbuf.at[:, 0], rz_self)
    att_out.wait()
    qg_out.wait()
    wait(zbuf, rz_recv)


def write_kernel(att_in, qg_in, zbuf, att, qg, kg, vg, buf, sem):
    cps = [pltpu.make_async_copy(att_in, att, sem.at[0]), pltpu.make_async_copy(qg_in, qg, sem.at[1])]
    for cp in cps:
        cp.start()
    for i, dst in enumerate((kg, vg)):
        for h in range(NZ):
            buf[i, pl.ds(h, 16, stride=8), :] = f32(zbuf[i, h])
        cps.append(pltpu.make_async_copy(buf.at[i], dst, sem.at[2 + i]))
        cps[-1].start()
    for cp in cps:
        cp.wait()


def on_device(queries, prefix_keys, prefix_values, out_grad, tile_mask, lengths):
    R = queries.shape[0] * queries.shape[1]
    S = 16 * BLK
    sm, hbm = pl.BlockSpec(memory_space=pltpu.SMEM), pl.BlockSpec(memory_space=pl.ANY)
    vmem, dma = pltpu.VMEM, pltpu.SemaphoreType.DMA
    rows = jax.ShapeDtypeStruct((R, 128), BF16)
    att, qg, heads = pl.pallas_call(
        kernel,
        out_shape=(rows, rows, jax.ShapeDtypeStruct((2, NZ, 16, 128), BF16)),
        in_specs=[sm, sm, hbm, hbm, hbm, hbm],
        out_specs=(hbm, hbm, pl.BlockSpec(memory_space=vmem)),
        scratch_shapes=[
            vmem((R, 128), BF16), vmem((R, 128), BF16), dma((2,)),
            vmem((16, 8, 128), BF16), vmem((16, 8, 128), BF16), vmem((R, 128), BF16), vmem((R, 128), BF16),
            vmem((2, 128, 128), F32), vmem((2, NZ, 16, 128), BF16), vmem((2, 4, 4, NZ, 32, 128), BF16),
            vmem((S, 256), BF16), vmem((S, 128), BF16), vmem((4, 8, BLK), F32),
            vmem((16, R, BLK), F32), vmem((16, R, BLK), F32), vmem((R, S), BF16),
            vmem((R, 128), F32), vmem((R, 128), F32), vmem((R, 128), F32),
            vmem((R, 128), F32), vmem((R, 256), F32),
            vmem((128, R), F32), vmem((128, R), F32), vmem((2, 128, R), BF16), vmem((2, 128, R), BF16),
            vmem((16, 2, NZ, 32, 128), BF16), vmem((16, 2, 4, 32, 128), BF16), vmem((3, 4, 2, 4, 32, 128), BF16),
            vmem((3, 2, 4, 32, 128), BF16), vmem((2, 4, 32, 128), BF16),
            dma((4,)), dma((2,)), dma((2,)), dma((2,)), dma((2, 3)), dma((2, 3)), dma((2, 3, 4)), dma((2, 3, 4)),
            dma((2, 4, 4)), dma((2, 4, 4)), dma((16,)), dma((16,)), dma((3, 4)), dma((3, 4)),
            dma((3,)), dma((3,)), dma, dma, dma,
        ],
        compiler_params=pltpu.CompilerParams(collective_id=0, has_side_effects=True,
                                             vmem_limit_bytes=60 * 2**20),
        name="shared_prompt",
    )(tile_mask, lengths, queries.reshape(R, 128), out_grad.reshape(R, 128), prefix_keys, prefix_values)
    grads = jax.ShapeDtypeStruct((128, 128), F32)
    att, qg, kg, vg = pl.pallas_call(
        write_kernel,
        out_shape=(rows, rows, grads, grads),
        in_specs=[pl.BlockSpec(memory_space=vmem)] * 3,
        out_specs=(hbm, hbm, hbm, hbm),
        scratch_shapes=[vmem((2, 128, 128), F32), dma((4,))],
        name="write_out",
    )(att, qg, heads)
    shape = prefix_keys.shape
    return att.reshape(queries.shape), qg.reshape(queries.shape), kg.reshape(shape), vg.reshape(shape)


def solution(mesh):
    tokens, owned = P("prefix", "group", None), P(("group", "prefix"), None, None)
    return jax.shard_map(
        on_device,
        mesh=mesh,
        in_specs=(tokens, owned, owned, tokens, P(), P()),
        out_specs=(tokens, tokens, owned, owned),
        check_vma=False,
    )
```
